32 devices in a mesh: expert: 4 (over y, x), replica: 8 (over z, core).
Axes of the slice: x: 2, y: 2, z: 4, core: 2. Of those that a mesh axis runs over, the one named last changes fastest.
Arguments:
- tokens: bfloat16 [4096, 2560], P(('expert', 'replica')), may hold values from -6 to 6
- cotangent: bfloat16 [4096, 2560], P(('expert', 'replica')), may hold values from -4 to 4
- partner: int32 [4096, 1], P(('expert', 'replica')), may hold values from 0 to 3; in each aligned block of 128 rows (0 to 127, 128 to 255, ...) at most 40 rows name the same one
- combine: int32 [4096, 2], P(('expert', 'replica')), may hold values from 1 to 8
- counts: int32 [32], P(('expert', 'replica')), may hold values from 32 to 128, as said below
- w_gate: bfloat16 [4, 2560, 768], P('expert', 'replica'), may hold values from -0.125 to 0.125
- w_up: bfloat16 [4, 2560, 768], P('expert', 'replica'), may hold values from -0.125 to 0.125
- w_down: bfloat16 [4, 768, 2560], P('expert', 'replica'), may hold values from -0.21875 to 0.21875
Outputs:
- token_grad: bfloat16 [4096, 2560], P(('expert', 'replica'))
- grad_down: bfloat16 [4, 768, 2560], P('expert', 'replica')
The draws below stay inside these ranges and needn't reach their ends.
Inputs may be any that keep to these rules, and one draw needn't show every extreme that they name: `partner`: within the 128 rows of one device no expert index is named by more than 40 rows, and some device names one exactly 40 times. `counts`: some device has all 128 slots real.
All inputs are finite; a program needn't handle non-finite values.
Results may differ from the reference program's by a relative error of at most 0.017.
Values may be sent and summed in bfloat16 or wider, within the bound.
A program may use at most 64 MiB of HBM per device.

```python
import math
import jax
import jax.numpy as jnp
import numpy as np
from jax import lax

D = 2560
H = 768
TOK_DEV = 128
CAP = 40
EXPERTS = 4
SHARDS = 32
TOKENS = 4096
N_EXPERT = 4
N_REPLICA = 8


def draw_counts(key, part):
    base = jax.random.randint(key, (SHARDS,), TOK_DEV // 4, TOK_DEV + 1)
    chosen = jax.random.randint(jax.random.fold_in(key, 7), (), 0, SHARDS)
    return jnp.where(jnp.arange(SHARDS) == chosen, TOK_DEV, base).astype(jnp.int32)


def touch_ends(entries, rng, low, high):
    index_at = [jax.random.randint(jax.random.fold_in(rng, axis), (), 0, length) for axis, length in enumerate(entries.shape)]
    main_axis = entries.shape.index(max(entries.shape))
    next_to = index_at[:main_axis] + [(index_at[main_axis] + 1) % entries.shape[main_axis]] + index_at[main_axis + 1:]
    return entries.at[tuple(index_at)].set(low).at[tuple(next_to)].set(high)


def level_of(own_key, shape, cuts, low, top_value):
    factor_of, own = 1.0, jax.random.fold_in(own_key, 6)
    for dim, parts in cuts:
        steps = jnp.exp(jax.random.uniform(jax.random.fold_in(own, dim), (parts,), jnp.float32, low / len(cuts), top_value / len(cuts)))
        factor_of = factor_of * jnp.repeat(steps, shape[dim] // parts).reshape([-1 if axis == dim else 1 for axis in range(len(shape))])
    return factor_of


def shared_out(rng, own, number, rows, number_of, top, limit, slope):
    order = jax.random.permutation(rng, number_of)
    packed, usual = shares(number_of, rows * top, limit, slope, True), shares(number_of, rows * top, limit, slope, False)
    places = jnp.arange(number_of)

    def named(tallies, rotation):
        used = int((tallies > 0).sum())
        fixed = max(1, used // 4)
        passed = fixed + (places - fixed + rotation * (used - fixed)) % max(1, number_of - fixed)
        return jnp.zeros((number_of,), jnp.int32).at[order[jnp.where(places < fixed, places, passed)]].set(jnp.asarray(tallies, jnp.int32))

    tallies = jnp.where(number % 4 == 0, named(packed, number // 4), named(usual, number - number // 4 - 1))
    mixed = jax.random.permutation(jax.random.fold_in(own, 3), number_of)
    donor, receiver = mixed[0:number_of // 2 * 2:2], mixed[1:number_of // 2 * 2:2]
    margin = jnp.minimum(tallies[donor] - 1, limit - tallies[receiver]) // 2
    margin = jnp.where((donor == order[0]) | (receiver == order[0]) | (tallies[receiver] == 0), 0, jnp.maximum(margin, 0))
    passed = jax.random.randint(jax.random.fold_in(own, 4), (number_of // 2,), 0, 1 << 20) % (margin + 1)
    tallies = tallies.at[donor].add(-passed).at[receiver].add(passed)
    items = jnp.searchsorted(jnp.cumsum(tallies), jnp.arange(rows * top), side="right").astype(jnp.int32)
    table = items.reshape(top, rows).T
    table = table[jax.random.permutation(jax.random.fold_in(own, 1), rows)]
    rotation = jax.random.randint(jax.random.fold_in(own, 2), (rows, 1), 0, top)
    return jnp.take_along_axis(table, (jnp.arange(top)[None, :] + rotation) % top, axis=1)


def shares(amount, total, bound, lean, full):
    loads = [(1 << 20) // math.isqrt(standing ** lean) + 1 for standing in range(1, amount + 1)]
    largest = bound if full else min(bound, max(-(-total // amount), total * loads[0] // sum(loads)))
    least = 1 if total - largest >= amount - 1 else 0
    given, surplus = [largest] + [least] * (amount - 1), total - largest - least * (amount - 1)
    while surplus > 0:
        candidates = [i for i in range(1, amount) if given[i] < largest] or [i for i in range(1, amount) if given[i] < bound]
        whole, remaining = sum([loads[i] for i in candidates]), surplus
        for i in candidates:
            extra = min(bound - given[i], max(1, remaining * loads[i] // whole), surplus)
            given[i] = given[i] + extra
            surplus = surplus - extra
    return np.array(given)


def gaussian(own_key, shape, scale, bound, shards=(), kind=jnp.bfloat16):
    drawn = jax.random.normal(own_key, shape, jnp.float32) * scale
    if len(shards) > 0:
        drawn = level_of(own_key, shape, shards, -0.22, 0.18) * drawn
    return jnp.clip(drawn, min=-bound, max=bound).astype(kind)


def setup_inputs(seed: int = 0) -> dict:
    key_list = jax.random.split(jax.random.key(seed), 9)
    tokens = gaussian(key_list[0], (TOKENS, D), 1.0, 6.0, ((0, 32),))
    cotangent = gaussian(key_list[1], (TOKENS, D), 0.5, 4.0, ((0, 32),))
    partner_keys = jax.random.split(jax.random.fold_in(key_list[2], 1), TOKENS // TOK_DEV)
    partner_turns = jax.random.permutation(jax.random.fold_in(key_list[2], 3), TOKENS // TOK_DEV)
    partner = jax.vmap(lambda own, number: shared_out(jax.random.fold_in(key_list[2], 2), own, number, TOK_DEV, N_EXPERT, 1, CAP, 2))(partner_keys, partner_turns).reshape((TOKENS, 1))
    combine = touch_ends(jax.random.randint(key_list[3], (TOKENS, 2), 1, 9), jax.random.fold_in(key_list[3], 1), 1, 8).astype(jnp.int32)
    counts = draw_counts(jax.random.fold_in(key_list[8], 71), 0)
    w_gate = gaussian(key_list[5], (EXPERTS, D, H), D ** -0.5, 0.125, ((0, 4), (1, 8)))
    w_up = gaussian(key_list[6], (EXPERTS, D, H), D ** -0.5, 0.125, ((0, 4), (1, 8)))
    w_down = gaussian(key_list[7], (EXPERTS, H, D), H ** -0.5, 0.21875, ((0, 4), (1, 8)))
    return dict(tokens=tokens, cotangent=cotangent, partner=partner, combine=combine, counts=counts, w_gate=w_gate, w_up=w_up, w_down=w_down)


def expert_backward(inputs, upstream, gate_w, up_w, down_w):
    gate_act = jnp.dot(inputs, gate_w, preferred_element_type=jnp.float32)
    up_act = jnp.dot(inputs, up_w, preferred_element_type=jnp.float32)
    sigmoid_gate = jax.nn.sigmoid(gate_act)
    swish_gate = gate_act * sigmoid_gate
    hidden = (swish_gate * up_act).astype(jnp.bfloat16)
    hidden_grad = jnp.dot(upstream, down_w.T, preferred_element_type=jnp.float32)
    gate_grad = (hidden_grad * up_act * sigmoid_gate * (1.0 + gate_act * (1.0 - sigmoid_gate))).astype(jnp.bfloat16)
    up_grad = (hidden_grad * swish_gate).astype(jnp.bfloat16)
    input_grad = jnp.dot(gate_grad, gate_w.T, preferred_element_type=jnp.float32) + jnp.dot(up_grad, up_w.T, preferred_element_type=jnp.float32)
    return hidden, input_grad


def reference(tokens, cotangent, partner, combine, counts, w_gate, w_up, w_down):
    token_ids = jnp.arange(TOKENS, dtype=jnp.int32)
    device_ids = token_ids // TOK_DEV
    valid_rows = (token_ids % TOK_DEV) < counts[device_ids]
    weights = combine.astype(jnp.float32)
    weight_sum = weights[:, 0] + weights[:, 1]
    share_home = jnp.where(valid_rows, weights[:, 0] / weight_sum, 0.0)
    share_away = jnp.where(valid_rows, weights[:, 1] / weight_sum, 0.0)
    upstream = cotangent.astype(jnp.float32)
    q_home = (upstream * share_home[:, None]).astype(jnp.bfloat16)
    q_away = (upstream * share_away[:, None]).astype(jnp.bfloat16)
    target = partner[:, 0].astype(jnp.int32)
    onehot_rows = (target.reshape(SHARDS, TOK_DEV)[:, :, None] == jnp.arange(N_EXPERT, dtype=jnp.int32)[None, None, :]).astype(jnp.int32)
    rank_within = jnp.sum((jnp.cumsum(onehot_rows, axis=1) - onehot_rows) * onehot_rows, axis=2).reshape(TOKENS).astype(jnp.int32)
    slot_index = (device_ids * CAP + rank_within).astype(jnp.int32)
    slot_table = jnp.full((N_EXPERT, SHARDS * CAP), TOKENS, dtype=jnp.int32).at[target, slot_index].set(token_ids)
    padded_x = jnp.concatenate([tokens, jnp.zeros((1, D), tokens.dtype)], axis=0)
    padded_q = jnp.concatenate([q_away, jnp.zeros((1, D), q_away.dtype)], axis=0)
    home_x = tokens.reshape(N_EXPERT, N_REPLICA * TOK_DEV, D)
    home_q = q_home.reshape(N_EXPERT, N_REPLICA * TOK_DEV, D)

    def per_expert(operands):
        x_home, q_here, slots, gate_w, up_w, down_w = operands
        hidden_home, grad_home = expert_backward(x_home, q_here, gate_w, up_w, down_w)
        x_away = jnp.take(padded_x, slots, axis=0)
        q_there = jnp.take(padded_q, slots, axis=0)
        hidden_away, grad_away = expert_backward(x_away, q_there, gate_w, up_w, down_w)
        part_home = jnp.einsum("rth,rtd->rhd", hidden_home.reshape(N_REPLICA, TOK_DEV, H).astype(jnp.float32), q_here.reshape(N_REPLICA, TOK_DEV, D).astype(jnp.float32))
        part_away = jnp.einsum("srch,srcd->rhd", hidden_away.reshape(N_EXPERT, N_REPLICA, CAP, H).astype(jnp.float32), q_there.reshape(N_EXPERT, N_REPLICA, CAP, D).astype(jnp.float32))
        partial_grad = lax.optimization_barrier((part_home + part_away).astype(jnp.bfloat16))
        grad_down = jnp.sum(partial_grad.astype(jnp.float32), axis=0).astype(jnp.bfloat16)
        return grad_home, grad_away.astype(jnp.bfloat16), grad_down

    grad_home_all, grad_away_all, grad_down = lax.map(per_expert, (home_x, home_q, slot_table, w_gate, w_up, w_down))
    grad_home_flat = grad_home_all.reshape(TOKENS, D)
    grad_away_flat = grad_away_all[target, slot_index]
    token_grad = (grad_home_flat + grad_away_flat.astype(jnp.float32)).astype(jnp.bfloat16)
    return token_grad, grad_down
```

```python
import functools

import jax
import jax.numpy as jnp
from jax import lax
from jax.experimental import pallas as pl
from jax.experimental.pallas import tpu as pltpu
from jax.sharding import PartitionSpec as P

BF16 = jnp.bfloat16
F32 = jnp.float32
MESH = pl.DeviceIdType.MESH
TILE = 256


def dot(left, right):
    return jnp.dot(left, right, preferred_element_type=F32)


def dot_rows(left, right):
    return lax.dot_general(
        left, right, (((1,), (1,)), ((), ())), preferred_element_type=F32
    )


def each(start, stop, body):
    def step(i, carry):
        body(i)
        return carry

    lax.fori_loop(start, stop, step, 0)


def kernel(
    experts, stages, cores, cap,
    tok_ref, cot_ref, partner_ref, combine_ref, counts_ref, wg_ref, wu_ref, wd_ref,
    grad_ref, down_ref,
    wg, wu, wd, x_all, q_all, send_x, send_q, gate_act, up_act, hid, hid_t,
    gate_grad, up_grad, home, back_send, back_recv, place_t,
    own_sum, pair_send, pair_recv, sum_send, sum_recv,
    w_local, w_send, w_recv, w_pair_send, w_pair_recv,
    row_send, row_recv, row_local, back_send_sem, back_recv_sem, back_local,
    pair_send_sem, pair_recv_sem, sum_send_sem, sum_recv_sem,
):
    rows = tok_ref.shape[0]
    width = tok_ref.shape[1]
    away = experts * cap
    total = rows + away
    padded = hid.shape[0]
    units = wd.shape[0]
    shard = wd_ref.shape[1]
    me_e = lax.axis_index("expert")
    me_r = lax.axis_index("replica")
    z = me_r // cores
    core = me_r % cores
    sources = (wg_ref, wu_ref, wd_ref)
    stores = (wg, wu, wd)

    def at_stage(stage):
        return (me_e, stage * cores + core)

    sibling = (me_e, z * cores + (cores - 1 - core))

    barrier = pltpu.get_barrier_semaphore()

    def greet(device):
        pl.semaphore_signal(barrier, inc=1, device_id=device, device_id_type=MESH)

    @pl.when(z > 0)
    def _():
        greet(at_stage(z - 1))

    @pl.when(z < stages - 1)
    def _():
        greet(at_stage(z + 1))

    if cores == 2:
        greet(sibling)

    each(1, experts, lambda i: greet(((me_e + i) % experts, me_r)))
    ends = jnp.where(z > 0, 1, 0) + jnp.where(z < stages - 1, 1, 0)
    pl.semaphore_wait(barrier, ends + (cores - 1) + (experts - 1))

    def part(kind, stage, owner_core):
        length = sources[kind].shape[1]
        begin = pl.multiple_of((stage * cores + owner_core) * length, 16)
        return stores[kind].at[pl.ds(begin, length)]

    def along(kind, stage, way, own=False):
        return pltpu.make_async_remote_copy(
            src_ref=sources[kind].at[0] if own else part(kind, stage, core),
            dst_ref=part(kind, stage, core),
            send_sem=w_send.at[kind, stage, way],
            recv_sem=w_recv.at[kind, stage],
            device_id=at_stage(z - 1 if way == 0 else z + 1),
            device_id_type=MESH,
        )

    def across(kind, stage, own=False, owner=None):
        owner = core if owner is None else owner
        return pltpu.make_async_remote_copy(
            src_ref=sources[kind].at[0] if own else part(kind, stage, owner),
            dst_ref=part(kind, stage, owner),
            send_sem=w_pair_send.at[kind, stage],
            recv_sem=w_pair_recv.at[kind, stage],
            device_id=sibling,
            device_id_type=MESH,
        )

    def local_weight(kind):
        return pltpu.make_async_copy(
            sources[kind].at[0], part(kind, z, core), w_local.at[kind]
        )

    def start_down(k):
        @pl.when((z > 0) & (stages - 1 - z == k))
        def _():
            along(2, z, 0, True).start()

        @pl.when((z < stages - 1) & (z == k))
        def _():
            along(2, z, 1, True).start()

    for kind in (0, 1):
        @pl.when(z > 0)
        def _():
            along(kind, z, 0, True).start()

        @pl.when(z < stages - 1)
        def _():
            along(kind, z, 1, True).start()

    start_down(0)
    for kind in range(3):
        if cores == 2:
            across(kind, z, True).start()
        local_weight(kind).start()

    def pass_on(kind, k):
        @pl.when(z - k >= 0)
        def _():
            along(kind, z - k, 1).wait_recv()

            @pl.when(z < stages - 1)
            def _():
                along(kind, z - k, 1).start()

            if cores == 2:
                across(kind, z - k).start()

        @pl.when(z + k < stages)
        def _():
            along(kind, z + k, 0).wait_recv()

            @pl.when(z > 0)
            def _():
                along(kind, z + k, 0).start()

            if cores == 2:
                across(kind, z + k).start()

    ratios = combine_ref[...].astype(F32)
    ratio_sum = ratios[:, 0:1] + ratios[:, 1:2]
    real = lax.broadcasted_iota(jnp.int32, (rows, 1), 0) < counts_ref[...]
    share_home = jnp.where(real, ratios[:, 0:1] / ratio_sum, 0.0)
    share_away = jnp.where(real, ratios[:, 1:2] / ratio_sum, 0.0)
    lanes = 128
    partner = partner_ref[...]
    chosen = partner == lax.broadcasted_iota(jnp.int32, (rows, lanes), 1)
    chosen = jnp.where(chosen, 1.0, 0.0)
    earlier = lax.broadcasted_iota(jnp.int32, (rows, rows), 0) > lax.broadcasted_iota(
        jnp.int32, (rows, rows), 1
    )
    earlier = jnp.where(earlier, 1.0, 0.0).astype(BF16)
    rank = jnp.sum(dot(earlier, chosen.astype(BF16)) * chosen, axis=1, keepdims=True)
    slot = partner.astype(F32) * cap + rank
    slot_row = jnp.transpose(jnp.broadcast_to(slot, (rows, lanes)))[0:1, :]
    place_t[...] = jnp.where(
        slot == lax.broadcasted_iota(jnp.int32, (rows, away), 1).astype(F32), 1.0, 0.0
    ).astype(BF16)
    place = jnp.where(
        slot_row == lax.broadcasted_iota(jnp.int32, (away, rows), 0).astype(F32), 1.0, 0.0
    ).astype(BF16)

    def prepare(i):
        cols = pl.ds(pl.multiple_of(i * TILE, TILE), TILE)
        x = tok_ref[:, cols]
        upstream = cot_ref[:, cols].astype(F32)
        x_all[0:rows, cols] = x
        q_all[0:rows, cols] = (upstream * share_home).astype(BF16)
        send_x[:, cols] = dot(place, x).astype(BF16)
        send_q[:, cols] = dot(place, (upstream * share_away).astype(BF16)).astype(BF16)
        if padded > total:
            q_all[total:padded, cols] = jnp.zeros((padded - total, TILE), BF16)

    each(0, width // TILE, prepare)

    def slots(index, base=0):
        return pl.ds(pl.multiple_of(base + index * cap, 16), cap)

    def row_copy(which, other, block):
        return pltpu.make_async_remote_copy(
            src_ref=(send_x, send_q)[which].at[slots(other)],
            dst_ref=(x_all, q_all)[which].at[slots(block, rows)],
            send_sem=row_send.at[which, other],
            recv_sem=row_recv.at[which, block],
            device_id=(other, me_r),
            device_id_type=MESH,
        )

    def row_copy_local(which):
        return pltpu.make_async_copy(
            (send_x, send_q)[which].at[slots(me_e)],
            (x_all, q_all)[which].at[slots(me_e, rows)],
            row_local.at[which],
        )

    for which in (0, 1):
        each(1, experts, lambda i: row_copy(which, (me_e + i) % experts, me_e).start())
        row_copy_local(which).start()

    def first_weights(k):
        pass_on(0, k)
        pass_on(1, k)
        start_down(k)

    each(1, stages, first_weights)

    for which in (0, 1):
        def arrive(i):
            other = (me_e + i) % experts
            row_copy(which, other, other).wait_recv()

        each(1, experts, arrive)
        row_copy_local(which).wait()
    for kind in (0, 1):
        local_weight(kind).wait()
        if cores == 2:
            each(0, stages, lambda s: across(kind, s, owner=1 - core).wait_recv())

    if padded > total:
        hid[total:padded, :] = jnp.zeros((padded - total, TILE), F32)

    def forward(i):
        cols = pl.ds(pl.multiple_of(i * TILE, TILE), TILE)
        x = x_all[...]
        gate = dot(x, wg[:, cols])
        up = dot(x, wu[:, cols])
        gate_act[:, cols] = gate
        up_act[:, cols] = up
        hid[0:total, :] = gate * jax.nn.sigmoid(gate) * up
        hid_t[cols, :] = jnp.transpose(hid[...]).astype(BF16)

    each(0, units // TILE, forward)

    def partial(stage, owner_core):
        begin = pl.multiple_of((stage * cores + owner_core) * shard, 16)
        return dot(hid_t[pl.ds(begin, shard), :], q_all[...])

    def pair_copy(stage):
        return pltpu.make_async_remote_copy(
            src_ref=pair_send.at[stage],
            dst_ref=pair_recv.at[stage],
            send_sem=pair_send_sem.at[stage],
            recv_sem=pair_recv_sem.at[stage],
            device_id=sibling,
            device_id_type=MESH,
        )

    if cores == 2:
        def for_sibling(stage):
            pair_send[stage] = partial(stage, 1 - core).astype(BF16)
            pair_copy(stage).start()

        each(0, stages, for_sibling)

    def for_own(stage):
        mine = partial(stage, core)
        if cores == 2:
            pair_copy(stage).wait_recv()
            mine = mine + pair_recv[stage].astype(F32)
        own_sum[stage] = mine

    each(0, stages, for_own)

    def sum_copy(target, way):
        there = z - 1 if way == 0 else z + 1
        slot_there = target if way == 0 else jnp.where(target == there, stages, target)
        return pltpu.make_async_remote_copy(
            src_ref=sum_send.at[target],
            dst_ref=sum_recv.at[slot_there],
            send_sem=sum_send_sem.at[target],
            recv_sem=sum_recv_sem.at[slot_there],
            device_id=at_stage(there),
            device_id_type=MESH,
        )

    def sum_arrived(slot_here):
        pltpu.make_async_remote_copy(
            src_ref=sum_send.at[0],
            dst_ref=sum_recv.at[slot_here],
            send_sem=sum_send_sem.at[0],
            recv_sem=sum_recv_sem.at[slot_here],
            device_id=at_stage(jnp.where(z > 0, z - 1, z + 1)),
            device_id_type=MESH,
        ).wait_recv()

    def chain(j, at_end):
        low, high = j, stages - 1 - j

        @pl.when((low < z) & ((z == stages - 1) == at_end))
        def _():
            value = own_sum[low]
            if not at_end:
                sum_arrived(low)
                value = value + sum_recv[low].astype(F32)
            sum_send[low] = value.astype(BF16)
            sum_copy(low, 0).start()

        @pl.when((high > z) & ((z == 0) == at_end))
        def _():
            value = own_sum[high]
            if not at_end:
                sum_arrived(high)
                value = value + sum_recv[high].astype(F32)
            sum_send[high] = value.astype(BF16)
            sum_copy(high, 1).start()

    each(0, stages, lambda j: chain(j, True))

    each(1, stages, lambda k: pass_on(2, k))
    local_weight(2).wait()
    if cores == 2:
        each(0, stages, lambda s: across(2, s, owner=1 - core).wait_recv())

    def backward(i):
        cols = pl.ds(pl.multiple_of(i * TILE, TILE), TILE)
        hidden_grad = dot_rows(q_all[0:total, :], wd[cols, :])
        gate = gate_act[:, cols]
        s = jax.nn.sigmoid(gate)
        gate_grad[:, cols] = (
            hidden_grad * up_act[:, cols] * s * (1.0 + gate * (1.0 - s))
        ).astype(BF16)
        up_grad[:, cols] = (hidden_grad * (gate * s)).astype(BF16)

    each(0, units // TILE, backward)

    def inputs(i):
        cols = pl.ds(pl.multiple_of(i * TILE, TILE), TILE)
        value = dot_rows(gate_grad[...], wg[cols, :]) + dot_rows(up_grad[...], wu[cols, :])
        home[:, cols] = value[0:rows]
        back_send[:, cols] = value[rows:total].astype(BF16)

    each(0, width // TILE, inputs)

    def back_copy(other, block):
        return pltpu.make_async_remote_copy(
            src_ref=back_send.at[slots(other)],
            dst_ref=back_recv.at[slots(block)],
            send_sem=back_send_sem.at[other],
            recv_sem=back_recv_sem.at[block],
            device_id=(other, me_r),
            device_id_type=MESH,
        )

    def back_copy_local():
        return pltpu.make_async_copy(
            back_send.at[slots(me_e)], back_recv.at[slots(me_e)], back_local
        )

    each(1, experts, lambda i: back_copy((me_e + i) % experts, me_e).start())
    back_copy_local().start()

    each(0, stages, lambda j: chain(j, False))

    def back_arrive(i):
        other = (me_e + i) % experts
        back_copy(other, other).wait_recv()

    each(1, experts, back_arrive)
    back_copy_local().wait()

    def finish(i):
        cols = pl.ds(pl.multiple_of(i * TILE, TILE), TILE)
        grad_ref[:, cols] = (
            home[:, cols] + dot(place_t[...], back_recv[:, cols])
        ).astype(BF16)

    each(0, width // TILE, finish)

    @pl.when(z < stages - 1)
    def _():
        sum_arrived(z)
        own_sum[z] = own_sum[z] + sum_recv[z].astype(F32)

    @pl.when(z > 0)
    def _():
        sum_arrived(stages)
        own_sum[z] = own_sum[z] + sum_recv[stages].astype(F32)

    down_ref[0] = own_sum[z].astype(BF16)

    for kind in range(3):
        def sent(stage):
            @pl.when((stage >= z) & (z > 0))
            def _():
                along(kind, stage, 0).wait_send()

            @pl.when((stage <= z) & (z < stages - 1))
            def _():
                along(kind, stage, 1).wait_send()

            if cores == 2:
                across(kind, stage).wait_send()

        each(0, stages, sent)
    for which in (0, 1):
        each(1, experts, lambda i: row_copy(which, (me_e + i) % experts, me_e).wait_send())
    each(1, experts, lambda i: back_copy((me_e + i) % experts, me_e).wait_send())

    def sums_sent(stage):
        if cores == 2:
            pair_copy(stage).wait_send()

        @pl.when(stage < z)
        def _():
            sum_copy(stage, 0).wait_send()

        @pl.when(stage > z)
        def _():
            sum_copy(stage, 1).wait_send()

    each(0, stages, sums_sent)


def local(cores, tokens, cotangent, partner, combine, counts, w_gate, w_up, w_down):
    rows, width = tokens.shape
    experts = lax.axis_size("expert")
    replicas = lax.axis_size("replica")
    stages = replicas // cores
    slots = max(2, (5 * rows // 4 + experts - 1) // experts)
    cap = -(-slots // 16) * 16
    away = experts * cap
    total = rows + away
    padded = -(-total // 128) * 128
    units = w_gate.shape[2]
    shard = w_down.shape[1]
    dma = pltpu.SemaphoreType.DMA
    pairs = stages if cores == 2 else 1
    in_vmem = pl.BlockSpec(memory_space=pltpu.VMEM)
    in_place = pl.BlockSpec(memory_space=pl.ANY)
    return pl.pallas_call(
        functools.partial(kernel, experts, stages, cores, cap),
        out_shape=(
            jax.ShapeDtypeStruct((rows, width), BF16),
            jax.ShapeDtypeStruct((1, shard, width), BF16),
        ),
        in_specs=[in_vmem] * 5 + [in_place] * 3,
        out_specs=(in_vmem, in_vmem),
        scratch_shapes=[
            pltpu.VMEM((width, units), BF16),
            pltpu.VMEM((width, units), BF16),
            pltpu.VMEM((units, width), BF16),
            pltpu.VMEM((total, width), BF16),
            pltpu.VMEM((padded, width), BF16),
            pltpu.VMEM((away, width), BF16),
            pltpu.VMEM((away, width), BF16),
            pltpu.VMEM((total, units), F32),
            pltpu.VMEM((total, units), F32),
            pltpu.VMEM((padded, TILE), F32),
            pltpu.VMEM((units, padded), BF16),
            pltpu.VMEM((total, units), BF16),
            pltpu.VMEM((total, units), BF16),
            pltpu.VMEM((rows, width), F32),
            pltpu.VMEM((away, width), BF16),
            pltpu.VMEM((away, width), BF16),
            pltpu.VMEM((rows, away), BF16),
            pltpu.VMEM((stages, shard, width), F32),
            pltpu.VMEM((pairs, shard, width), BF16),
            pltpu.VMEM((pairs, shard, width), BF16),
            pltpu.VMEM((stages, shard, width), BF16),
            pltpu.VMEM((stages + 1, shard, width), BF16),
            dma((3,)),
            dma((3, stages, 2)),
            dma((3, stages)),
            dma((3, stages)),
            dma((3, stages)),
            dma((2, experts)),
            dma((2, experts)),
            dma((2,)),
            dma((experts,)),
            dma((experts,)),
            dma,
            dma((stages,)),
            dma((stages,)),
            dma((stages,)),
            dma((stages + 1,)),
        ],
        compiler_params=pltpu.CompilerParams(
            collective_id=0,
            has_side_effects=True,
            vmem_limit_bytes=60 * 2**20,
        ),
        cost_estimate=pl.CostEstimate(
            flops=12 * total * width * units,
            bytes_accessed=8 * rows * width + 6 * units * width,
            transcendentals=2 * total * units,
        ),
        name="expert_backward",
    )(tokens, cotangent, partner, combine, counts.reshape(1, 1), w_gate, w_up, w_down)


def cores_together(mesh):
    replicas = mesh.shape["replica"]
    if replicas % 2:
        return 1
    line = list(mesh.devices.reshape(-1)[:2])
    places = [getattr(device, "coords", None) for device in line]
    if None in places:
        return 2
    return 2 if tuple(places[0]) == tuple(places[1]) else 1


def solution(mesh):
    placed = (
        P(("expert", "replica"), None),
        P(("expert", "replica"), None),
        P(("expert", "replica"), None),
        P(("expert", "replica"), None),
        P(("expert", "replica")),
        P("expert", "replica", None),
        P("expert", "replica", None),
        P("expert", "replica", None),
    )
    return jax.shard_map(
        functools.partial(local, cores_together(mesh)),
        mesh=mesh,
        in_specs=placed,
        out_specs=(P(("expert", "replica"), None), P("expert", "replica", None)),
        check_vma=False,
    )
```

```python
import functools

import jax
import jax.numpy as jnp
from jax import lax
from jax.experimental import pallas as pl
from jax.experimental.pallas import tpu as pltpu
from jax.sharding import PartitionSpec as P

BF16 = jnp.bfloat16
F32 = jnp.float32
MESH = pl.DeviceIdType.MESH
TILE = 256


def dot(left, right):
    return jnp.dot(left, right, preferred_element_type=F32)


def dot_rows(left, right):
    return lax.dot_general(
        left, right, (((1,), (1,)), ((), ())), preferred_element_type=F32
    )


def each(start, stop, body):
    def step(i, carry):
        body(i)
        return carry

    lax.fori_loop(start, stop, step, 0)


def kernel(
    experts, stages, cores, cap, hosting,
    tok_ref, cot_ref, partner_ref, combine_ref, counts_ref, wg_ref, wu_ref, wd_ref,
    grad_ref, down_ref,
    wg, wu, wd, x_all, q_all, send_x, send_q, gate_act, up_act, hid, hid_t,
    gate_grad, up_grad, home, back_send, back_recv, place_t,
    own_sum, pair_sum, pair_send, pair_recv, sum_send, sum_recv,
    guest_q, guest_hid_t, guest_grad, hosted_grad,
    w_local, w_send, w_recv, w_pair_send, w_pair_recv,
    row_send, row_recv, row_local, back_send_sem, back_recv_sem, back_local,
    pair_send_sem, pair_recv_sem, sum_send_sem, sum_recv_sem,
    guest_send, guest_recv, hosted_send, hosted_recv,
):
    rows = tok_ref.shape[0]
    width = tok_ref.shape[1]
    away = experts * cap
    total = rows + away
    padded = hid.shape[0]
    units = wd.shape[0]
    shard = wd_ref.shape[1]
    me_e = lax.axis_index("expert")
    me_r = lax.axis_index("replica")
    z = me_r // cores
    core = me_r % cores
    sources = (wg_ref, wu_ref, wd_ref)
    stores = (wg, wu, wd)

    def at_stage(stage):
        return (me_e, stage * cores + core)

    sibling = (me_e, z * cores + (cores - 1 - core))
    first, last = (1, stages - 2) if hosting else (0, stages - 1)
    inner = (z >= first) & (z <= last)
    outer = (z < first) | (z > last)
    beside = jnp.where(z == 0, 1, jnp.where(z == stages - 1, stages - 2,
                       jnp.where(z == 1, 0, stages - 1)))

    def to_left(kind):
        return z > (first if kind == 2 else 0)

    def to_right(kind):
        return z < (last if kind == 2 else stages - 1)

    barrier = pltpu.get_barrier_semaphore()

    def greet(device):
        pl.semaphore_signal(barrier, inc=1, device_id=device, device_id_type=MESH)

    @pl.when(z > 0)
    def _():
        greet(at_stage(z - 1))

    @pl.when(z < stages - 1)
    def _():
        greet(at_stage(z + 1))

    if cores == 2:
        greet(sibling)

    each(1, experts, lambda i: greet(((me_e + i) % experts, me_r)))
    ends = jnp.where(z > 0, 1, 0) + jnp.where(z < stages - 1, 1, 0)
    pl.semaphore_wait(barrier, ends + (cores - 1) + (experts - 1))

    def part(kind, stage, owner_core):
        length = sources[kind].shape[1]
        begin = pl.multiple_of((stage * cores + owner_core) * length, 16)
        return stores[kind].at[pl.ds(begin, length)]

    def along(kind, stage, way, own=False):
        return pltpu.make_async_remote_copy(
            src_ref=sources[kind].at[0] if own else part(kind, stage, core),
            dst_ref=part(kind, stage, core),
            send_sem=w_send.at[kind, stage, way],
            recv_sem=w_recv.at[kind, stage],
            device_id=at_stage(z - 1 if way == 0 else z + 1),
            device_id_type=MESH,
        )

    def across(kind, stage, own=False, owner=None):
        owner = core if owner is None else owner
        return pltpu.make_async_remote_copy(
            src_ref=sources[kind].at[0] if own else part(kind, stage, owner),
            dst_ref=part(kind, stage, owner),
            send_sem=w_pair_send.at[kind, stage],
            recv_sem=w_pair_recv.at[kind, stage],
            device_id=sibling,
            device_id_type=MESH,
        )

    def local_weight(kind):
        return pltpu.make_async_copy(
            sources[kind].at[0], part(kind, z, core), w_local.at[kind]
        )

    def start_down(k):
        @pl.when(to_left(2) & (stages - 1 - z == k))
        def _():
            along(2, z, 0, True).start()

        @pl.when(to_right(2) & (z == k))
        def _():
            along(2, z, 1, True).start()

    for kind in (0, 1):
        @pl.when(z > 0)
        def _():
            along(kind, z, 0, True).start()

        @pl.when(z < stages - 1)
        def _():
            along(kind, z, 1, True).start()

    start_down(0)
    for kind in range(3):
        if cores == 2:
            @pl.when(inner | (kind < 2))
            def _():
                across(kind, z, True).start()

        local_weight(kind).start()

    def pass_on(kind, k):
        takes = inner | (kind < 2)

        @pl.when((z - k >= 0) & takes)
        def _():
            along(kind, z - k, 1).wait_recv()

            @pl.when(to_right(kind))
            def _():
                along(kind, z - k, 1).start()

            if cores == 2:
                across(kind, z - k).start()

        @pl.when((z + k < stages) & takes)
        def _():
            along(kind, z + k, 0).wait_recv()

            @pl.when(to_left(kind))
            def _():
                along(kind, z + k, 0).start()

            if cores == 2:
                across(kind, z + k).start()

    lanes = 128

    def column(row):
        return jnp.transpose(jnp.broadcast_to(row, (lanes, rows)))[:, 0:1]

    ratios = combine_ref[...].astype(F32)
    ratio_home, ratio_away = column(ratios[0:1, :]), column(ratios[1:2, :])
    ratio_sum = ratio_home + ratio_away
    real = lax.broadcasted_iota(jnp.int32, (rows, 1), 0) < counts_ref[...]
    share_home = jnp.where(real, ratio_home / ratio_sum, 0.0)
    share_away = jnp.where(real, ratio_away / ratio_sum, 0.0)
    partner = column(partner_ref[...].astype(F32))
    chosen = partner == lax.broadcasted_iota(jnp.int32, (rows, lanes), 1).astype(F32)
    chosen = jnp.where(chosen, 1.0, 0.0)
    earlier = lax.broadcasted_iota(jnp.int32, (rows, rows), 0) > lax.broadcasted_iota(
        jnp.int32, (rows, rows), 1
    )
    earlier = jnp.where(earlier, 1.0, 0.0).astype(BF16)
    rank = jnp.sum(dot(earlier, chosen.astype(BF16)) * chosen, axis=1, keepdims=True)
    slot = partner * cap + rank
    slot_row = jnp.transpose(jnp.broadcast_to(slot, (rows, lanes)))[0:1, :]
    place_t[...] = jnp.where(
        slot == lax.broadcasted_iota(jnp.int32, (rows, away), 1).astype(F32), 1.0, 0.0
    ).astype(BF16)
    place = jnp.where(
        slot_row == lax.broadcasted_iota(jnp.int32, (away, rows), 0).astype(F32), 1.0, 0.0
    ).astype(BF16)

    def prepare(i):
        cols = pl.ds(pl.multiple_of(i * TILE, TILE), TILE)
        x = tok_ref[:, cols]
        upstream = cot_ref[:, cols].astype(F32)
        x_all[0:rows, cols] = x
        q_all[0:rows, cols] = (upstream * share_home).astype(BF16)
        send_x[:, cols] = dot(place, x).astype(BF16)
        send_q[:, cols] = dot(place, (upstream * share_away).astype(BF16)).astype(BF16)
        if padded > total:
            q_all[total:padded, cols] = jnp.zeros((padded - total, TILE), BF16)
            if hosting:
                guest_q[total:padded, cols] = jnp.zeros((padded - total, TILE), BF16)

    each(0, width // TILE, prepare)

    def slots(index, base=0):
        return pl.ds(pl.multiple_of(base + index * cap, 16), cap)

    def row_copy(which, other, block):
        return pltpu.make_async_remote_copy(
            src_ref=(send_x, send_q)[which].at[slots(other)],
            dst_ref=(x_all, q_all)[which].at[slots(block, rows)],
            send_sem=row_send.at[which, other],
            recv_sem=row_recv.at[which, block],
            device_id=(other, me_r),
            device_id_type=MESH,
        )

    def row_copy_local(which):
        return pltpu.make_async_copy(
            (send_x, send_q)[which].at[slots(me_e)],
            (x_all, q_all)[which].at[slots(me_e, rows)],
            row_local.at[which],
        )

    for which in (0, 1):
        each(1, experts, lambda i: row_copy(which, (me_e + i) % experts, me_e).start())
        row_copy_local(which).start()

    def guest_copy(index):
        if index == 2:
            source, target = hid_t, guest_hid_t
        else:
            span = slice(0, rows) if index == 0 else slice(rows, total)
            source, target = q_all.at[span], guest_q.at[span]
        return pltpu.make_async_remote_copy(
            src_ref=source,
            dst_ref=target,
            send_sem=guest_send.at[index],
            recv_sem=guest_recv.at[index],
            device_id=at_stage(beside),
            device_id_type=MESH,
        )

    def hosted_copy():
        return pltpu.make_async_remote_copy(
            src_ref=guest_grad,
            dst_ref=hosted_grad,
            send_sem=hosted_send,
            recv_sem=hosted_recv,
            device_id=at_stage(beside),
            device_id_type=MESH,
        )

    def rows_arrive():
        for which in (1, 0):
            def arrive(i):
                other = (me_e + i) % experts
                row_copy(which, other, other).wait_recv()

            each(1, experts, arrive)
            row_copy_local(which).wait()
            if hosting and which == 1:
                @pl.when(outer)
                def _():
                    guest_copy(1).start()

    if hosting:
        @pl.when(outer)
        def _():
            guest_copy(0).start()
            rows_arrive()

    def first_weights(k):
        pass_on(0, k)
        pass_on(1, k)
        start_down(k)

    each(1, stages, first_weights)

    if hosting:
        pl.when(inner)(rows_arrive)
    else:
        rows_arrive()
    for kind in (0, 1):
        local_weight(kind).wait()
        if cores == 2:
            each(0, stages, lambda s: across(kind, s, owner=1 - core).wait_recv())

    if padded > total:
        hid[total:padded, :] = jnp.zeros((padded - total, TILE), F32)

    def forward(i):
        cols = pl.ds(pl.multiple_of(i * TILE, TILE), TILE)
        x = x_all[...]
        gate = dot(x, wg[:, cols])
        up = dot(x, wu[:, cols])
        gate_act[:, cols] = gate
        up_act[:, cols] = up
        hid[0:total, :] = gate * jax.nn.sigmoid(gate) * up
        hid_t[cols, :] = jnp.transpose(hid[...]).astype(BF16)

    each(0, units // TILE, forward)
    if hosting:
        @pl.when(outer)
        def _():
            guest_copy(2).start()

    def pair_copy(stage):
        return pltpu.make_async_remote_copy(
            src_ref=pair_send.at[stage],
            dst_ref=pair_recv.at[stage],
            send_sem=pair_send_sem.at[stage],
            recv_sem=pair_recv_sem.at[stage],
            device_id=sibling,
            device_id_type=MESH,
        )

    def partials():
        if hosting:
            guest_copy(2).wait_recv()

        def product(stage):
            length = cores * shard
            span = pl.ds(pl.multiple_of(stage * length, 16), length)

            def columns(i):
                cols = pl.ds(pl.multiple_of(i * 2 * TILE, TILE), 2 * TILE)
                value = dot(hid_t[span, :], q_all[:, cols])
                if hosting:
                    value = value + dot(guest_hid_t[span, :], guest_q[:, cols])
                for owner in range(cores):
                    pair_sum[owner, :, cols] = value[owner * shard : (owner + 1) * shard]

            each(0, width // (2 * TILE), columns)
            own_sum[stage] = pair_sum[core]
            if cores == 2:
                pair_send[stage] = pair_sum[1 - core].astype(BF16)
                pair_copy(stage).start()

        each(0, stages, product)
        if cores == 2:
            def joined(stage):
                pair_copy(stage).wait_recv()
                own_sum[stage] = own_sum[stage] + pair_recv[stage].astype(F32)

            each(0, stages, joined)

    def sum_copy(target, way):
        there = z - 1 if way == 0 else z + 1
        slot_there = target if way == 0 else jnp.where(target == there, stages, target)
        return pltpu.make_async_remote_copy(
            src_ref=sum_send.at[target],
            dst_ref=sum_recv.at[slot_there],
            send_sem=sum_send_sem.at[target],
            recv_sem=sum_recv_sem.at[slot_there],
            device_id=at_stage(there),
            device_id_type=MESH,
        )

    def sum_arrived(slot_here):
        pltpu.make_async_remote_copy(
            src_ref=sum_send.at[0],
            dst_ref=sum_recv.at[slot_here],
            send_sem=sum_send_sem.at[0],
            recv_sem=sum_recv_sem.at[slot_here],
            device_id=at_stage(jnp.where(z > 0, z - 1, z + 1)),
            device_id_type=MESH,
        ).wait_recv()

    def chain(j, at_end):
        low, high = j, stages - 1 - j

        @pl.when((low < z) & ((z == last) == at_end) & inner)
        def _():
            value = own_sum[low]
            if not at_end:
                sum_arrived(low)
                value = value + sum_recv[low].astype(F32)
            sum_send[low] = value.astype(BF16)
            sum_copy(low, 0).start()

        @pl.when((high > z) & ((z == first) == at_end) & inner)
        def _():
            value = own_sum[high]
            if not at_end:
                sum_arrived(high)
                value = value + sum_recv[high].astype(F32)
            sum_send[high] = value.astype(BF16)
            sum_copy(high, 1).start()

    if not hosting:
        partials()
        each(0, stages, lambda j: chain(j, True))

    each(1, stages, lambda k: pass_on(2, k))
    local_weight(2).wait()
    if cores == 2:
        @pl.when(inner)
        def _():
            each(0, stages, lambda s: across(2, s, owner=1 - core).wait_recv())

    def backward(i, hosted=False):
        cols = pl.ds(pl.multiple_of(i * TILE, TILE), TILE)
        if hosted:
            hidden_grad = hosted_grad[:, cols].astype(F32)
        else:
            hidden_grad = dot_rows(q_all[0:total, :], wd[cols, :])
        gate = gate_act[:, cols]
        s = jax.nn.sigmoid(gate)
        gate_grad[:, cols] = (
            hidden_grad * up_act[:, cols] * s * (1.0 + gate * (1.0 - s))
        ).astype(BF16)
        up_grad[:, cols] = (hidden_grad * (gate * s)).astype(BF16)

    def for_guest(i):
        cols = pl.ds(pl.multiple_of(i * TILE, TILE), TILE)
        guest_grad[:, cols] = dot_rows(guest_q[0:total, :], wd[cols, :]).astype(BF16)

    if hosting:
        @pl.when(inner)
        def _():
            guest_copy(0).wait_recv()
            guest_copy(1).wait_recv()
            each(0, units // TILE, for_guest)
            hosted_copy().start()
            each(0, units // TILE, backward)

        @pl.when(outer)
        def _():
            hosted_copy().wait_recv()
            each(0, units // TILE, lambda i: backward(i, True))
    else:
        each(0, units // TILE, backward)

    def inputs(i):
        cols = pl.ds(pl.multiple_of(i * TILE, TILE), TILE)
        value = dot_rows(gate_grad[...], wg[cols, :]) + dot_rows(up_grad[...], wu[cols, :])
        home[:, cols] = value[0:rows]
        back_send[:, cols] = value[rows:total].astype(BF16)

    half = width // 2

    def back_copy(part, other, block):
        cols = pl.ds(part * half, half)
        return pltpu.make_async_remote_copy(
            src_ref=back_send.at[slots(other), cols],
            dst_ref=back_recv.at[slots(block), cols],
            send_sem=back_send_sem.at[part, other],
            recv_sem=back_recv_sem.at[part, block],
            device_id=(other, me_r),
            device_id_type=MESH,
        )

    def back_copy_local(part):
        cols = pl.ds(part * half, half)
        return pltpu.make_async_copy(
            back_send.at[slots(me_e), cols],
            back_recv.at[slots(me_e), cols],
            back_local.at[part],
        )

    tiles = half // TILE
    for part_ in (0, 1):
        each(part_ * tiles, (part_ + 1) * tiles, inputs)
        each(1, experts, lambda i: back_copy(part_, (me_e + i) % experts, me_e).start())
        back_copy_local(part_).start()

    if hosting:
        pl.when(inner)(partials)
        each(0, stages, lambda j: chain(j, True))
    each(0, stages, lambda j: chain(j, False))

    def finish(i):
        cols = pl.ds(pl.multiple_of(i * TILE, TILE), TILE)
        grad_ref[:, cols] = (
            home[:, cols] + dot(place_t[...], back_recv[:, cols])
        ).astype(BF16)

    for part_ in (0, 1):
        def back_arrive(i):
            other = (me_e + i) % experts
            back_copy(part_, other, other).wait_recv()

        each(1, experts, back_arrive)
        back_copy_local(part_).wait()
        each(part_ * tiles, (part_ + 1) * tiles, finish)

    if hosting:
        @pl.when(outer)
        def _():
            own_sum[z] = jnp.zeros(own_sum.shape[1:], F32)

    @pl.when(z < last)
    def _():
        sum_arrived(z)
        own_sum[z] = own_sum[z] + sum_recv[z].astype(F32)

    @pl.when(z > first)
    def _():
        sum_arrived(stages)
        own_sum[z] = own_sum[z] + sum_recv[stages].astype(F32)

    down_ref[0] = own_sum[z].astype(BF16)

    for kind in range(3):
        def sent(stage):
            @pl.when((stage >= z) & to_left(kind))
            def _():
                along(kind, stage, 0).wait_send()

            @pl.when((stage <= z) & to_right(kind))
            def _():
                along(kind, stage, 1).wait_send()

            if cores == 2:
                @pl.when(inner | (kind < 2))
                def _():
                    across(kind, stage).wait_send()

        each(0, stages, sent)
    for which in (0, 1):
        each(1, experts, lambda i: row_copy(which, (me_e + i) % experts, me_e).wait_send())
        each(1, experts, lambda i: back_copy(which, (me_e + i) % experts, me_e).wait_send())

    def sums_sent(stage):
        if cores == 2:
            pair_copy(stage).wait_send()

        @pl.when(stage < z)
        def _():
            sum_copy(stage, 0).wait_send()

        @pl.when(stage > z)
        def _():
            sum_copy(stage, 1).wait_send()

    if hosting:
        @pl.when(inner)
        def _():
            each(0, stages, sums_sent)
            hosted_copy().wait_send()

        @pl.when(outer)
        def _():
            for index in range(3):
                guest_copy(index).wait_send()
    else:
        each(0, stages, sums_sent)


def local(cores, tokens, cotangent, partner, combine, counts, w_gate, w_up, w_down):
    rows, width = tokens.shape
    experts = lax.axis_size("expert")
    replicas = lax.axis_size("replica")
    stages = replicas // cores
    slots = max(2, (5 * rows // 4 + experts - 1) // experts)
    cap = -(-slots // 16) * 16
    away = experts * cap
    total = rows + away
    padded = -(-total // 128) * 128
    hosting = stages == 4
    units = w_gate.shape[2]
    shard = w_down.shape[1]
    dma = pltpu.SemaphoreType.DMA
    pairs = stages if cores == 2 else 1
    in_vmem = pl.BlockSpec(memory_space=pltpu.VMEM)
    in_place = pl.BlockSpec(memory_space=pl.ANY)
    return pl.pallas_call(
        functools.partial(kernel, experts, stages, cores, cap, hosting),
        out_shape=(
            jax.ShapeDtypeStruct((rows, width), BF16),
            jax.ShapeDtypeStruct((1, shard, width), BF16),
        ),
        in_specs=[in_vmem] * 5 + [in_place] * 3,
        out_specs=(in_vmem, in_vmem),
        scratch_shapes=[
            pltpu.VMEM((width, units), BF16),
            pltpu.VMEM((width, units), BF16),
            pltpu.VMEM((units, width), BF16),
            pltpu.VMEM((total, width), BF16),
            pltpu.VMEM((padded, width), BF16),
            pltpu.VMEM((away, width), BF16),
            pltpu.VMEM((away, width), BF16),
            pltpu.VMEM((total, units), F32),
            pltpu.VMEM((total, units), F32),
            pltpu.VMEM((padded, TILE), F32),
            pltpu.VMEM((units, padded), BF16),
            pltpu.VMEM((total, units), BF16),
            pltpu.VMEM((total, units), BF16),
            pltpu.VMEM((rows, width), F32),
            pltpu.VMEM((away, width), BF16),
            pltpu.VMEM((away, width), BF16),
            pltpu.VMEM((rows, away), BF16),
            pltpu.VMEM((stages, shard, width), F32),
            pltpu.VMEM((cores, shard, width), F32),
            pltpu.VMEM((pairs, shard, width), BF16),
            pltpu.VMEM((pairs, shard, width), BF16),
            pltpu.VMEM((stages, shard, width), BF16),
            pltpu.VMEM((stages + 1, shard, width), BF16),
            pltpu.VMEM((padded if hosting else 16, width), BF16),
            pltpu.VMEM((units if hosting else 16, padded), BF16),
            pltpu.VMEM((total if hosting else 16, units), BF16),
            pltpu.VMEM((total if hosting else 16, units), BF16),
            dma((3,)),
            dma((3, stages, 2)),
            dma((3, stages)),
            dma((3, stages)),
            dma((3, stages)),
            dma((2, experts)),
            dma((2, experts)),
            dma((2,)),
            dma((2, experts)),
            dma((2, experts)),
            dma((2,)),
            dma((stages,)),
            dma((stages,)),
            dma((stages,)),
            dma((stages + 1,)),
            dma((3,)),
            dma((3,)),
            dma,
            dma,
        ],
        compiler_params=pltpu.CompilerParams(
            collective_id=0,
            has_side_effects=True,
            vmem_limit_bytes=60 * 2**20,
        ),
        cost_estimate=pl.CostEstimate(
            flops=12 * total * width * units,
            bytes_accessed=8 * rows * width + 6 * units * width,
            transcendentals=2 * total * units,
        ),
        name="expert_backward",
    )(tokens, cotangent, partner.T, combine.T, counts.reshape(1, 1), w_gate, w_up, w_down)


def cores_together(mesh):
    replicas = mesh.shape["replica"]
    if replicas % 2:
        return 1
    line = list(mesh.devices.reshape(-1)[:2])
    places = [getattr(device, "coords", None) for device in line]
    if None in places:
        return 2
    return 2 if tuple(places[0]) == tuple(places[1]) else 1


def solution(mesh):
    placed = (
        P(("expert", "replica"), None),
        P(("expert", "replica"), None),
        P(("expert", "replica"), None),
        P(("expert", "replica"), None),
        P(("expert", "replica")),
        P("expert", "replica", None),
        P("expert", "replica", None),
        P("expert", "replica", None),
    )
    return jax.shard_map(
        functools.partial(local, cores_together(mesh)),
        mesh=mesh,
        in_specs=placed,
        out_specs=(P(("expert", "replica"), None), P("expert", "replica", None)),
        check_vma=False,
    )
```

```python
import functools

import jax
import jax.numpy as jnp
from jax import lax
from jax.experimental import pallas as pl
from jax.experimental.pallas import tpu as pltpu
from jax.sharding import PartitionSpec as P

BF16 = jnp.bfloat16
F32 = jnp.float32
MESH = pl.DeviceIdType.MESH
TILE = 256


def dot(left, right):
    return jnp.dot(left, right, preferred_element_type=F32)


def dot_rows(left, right):
    return lax.dot_general(
        left, right, (((1,), (1,)), ((), ())), preferred_element_type=F32
    )


def each(start, stop, body):
    def step(i, carry):
        body(i)
        return carry

    lax.fori_loop(start, stop, step, 0)


def kernel(
    experts, stages, cores, cap, hosting,
    tok_ref, cot_ref, partner_ref, combine_ref, counts_ref, wg_ref, wu_ref, wd_ref,
    grad_ref, down_ref,
    wg, wu, wd, x_all, q_all, send_x, send_q, gate_act, up_act, hid, hid_t,
    gate_grad, up_grad, home, back_send, back_recv, place_t,
    own_sum, pair_sum, pair_send, pair_recv, sum_send, sum_recv,
    guest_q, guest_hid_t, guest_grad, hosted_grad,
    w_local, w_send, w_recv, w_pair_send, w_pair_recv,
    row_send, row_recv, row_local, back_send_sem, back_recv_sem, back_local,
    pair_send_sem, pair_recv_sem, sum_send_sem, sum_recv_sem,
    guest_send, guest_recv, hosted_send, hosted_recv,
):
    rows = tok_ref.shape[0]
    width = tok_ref.shape[1]
    away = experts * cap
    total = rows + away
    padded = hid.shape[0]
    units = wd.shape[0]
    shard = wd_ref.shape[1]
    me_e = lax.axis_index("expert")
    me_r = lax.axis_index("replica")
    z = me_r // cores
    core = me_r % cores
    tiles_h = units // TILE
    tile_order = [0] + [tiles_h - 1] * (tiles_h > 1) + list(range(1, tiles_h - 1))
    pieces = [(which, tile) for tile in tile_order for which in (0, 1)] + [(2, 0)]
    down = len(pieces) - 1
    early = min(4, down)
    phases = (range(0, early), range(early, down), range(down, down + 1))

    def at_stage(stage):
        return (me_e, stage * cores + core)

    sibling = (me_e, z * cores + (cores - 1 - core))
    first, last = (1, stages - 2) if hosting else (0, stages - 1)
    inner = (z >= first) & (z <= last)
    outer = (z < first) | (z > last)
    beside = jnp.where(z == 0, 1, jnp.where(z == stages - 1, stages - 2,
                       jnp.where(z == 1, 0, stages - 1)))

    def to_left(kind):
        return z > (first if kind == down else 0)

    def to_right(kind):
        return z < (last if kind == down else stages - 1)

    barrier = pltpu.get_barrier_semaphore()

    def greet(device):
        pl.semaphore_signal(barrier, inc=1, device_id=device, device_id_type=MESH)

    @pl.when(z > 0)
    def _():
        greet(at_stage(z - 1))

    @pl.when(z < stages - 1)
    def _():
        greet(at_stage(z + 1))

    if cores == 2:
        greet(sibling)

    each(1, experts, lambda i: greet(((me_e + i) % experts, me_r)))
    ends = jnp.where(z > 0, 1, 0) + jnp.where(z < stages - 1, 1, 0)
    pl.semaphore_wait(barrier, ends + (cores - 1) + (experts - 1))

    def part(kind, stage, owner_core):
        which, tile = pieces[kind]
        length = (wg_ref, wu_ref, wd_ref)[which].shape[1]
        begin = pl.multiple_of((stage * cores + owner_core) * length, 16)
        span = pl.ds(begin, length)
        if kind == down:
            return wd.at[span]
        return (wg, wu)[which].at[span, pl.ds(tile * TILE, TILE)]

    def mine(kind):
        which, tile = pieces[kind]
        if kind == down:
            return wd_ref.at[0]
        return (wg_ref, wu_ref)[which].at[0, :, pl.ds(tile * TILE, TILE)]

    def along(kind, stage, way, own=False):
        return pltpu.make_async_remote_copy(
            src_ref=mine(kind) if own else part(kind, stage, core),
            dst_ref=part(kind, stage, core),
            send_sem=w_send.at[kind, stage, way],
            recv_sem=w_recv.at[kind, stage],
            device_id=at_stage(z - 1 if way == 0 else z + 1),
            device_id_type=MESH,
        )

    def across(kind, stage, own=False, owner=None):
        owner = core if owner is None else owner
        return pltpu.make_async_remote_copy(
            src_ref=mine(kind) if own else part(kind, stage, owner),
            dst_ref=part(kind, stage, owner),
            send_sem=w_pair_send.at[kind, stage],
            recv_sem=w_pair_recv.at[kind, stage],
            device_id=sibling,
            device_id_type=MESH,
        )

    def local_weight(kind):
        return pltpu.make_async_copy(
            mine(kind), part(kind, z, core), w_local.at[kind]
        )

    def start_own(phase, k):
        for kind in phases[phase]:
            @pl.when(to_left(kind) & (stages - 1 - z == k))
            def _():
                along(kind, z, 0, True).start()

            @pl.when(to_right(kind) & (z == k))
            def _():
                along(kind, z, 1, True).start()

    for kind in phases[0]:
        @pl.when(to_left(kind))
        def _():
            along(kind, z, 0, True).start()

        @pl.when(to_right(kind))
        def _():
            along(kind, z, 1, True).start()

    start_own(1, 0)
    start_own(2, 0)
    for kind in range(down + 1):
        if cores == 2:
            @pl.when(inner | (kind < down))
            def _():
                across(kind, z, True).start()

        local_weight(kind).start()

    def pass_on(kind, k):
        takes = inner | (kind < down)

        @pl.when((z - k >= 0) & takes)
        def _():
            along(kind, z - k, 1).wait_recv()

            @pl.when(to_right(kind))
            def _():
                along(kind, z - k, 1).start()

            if cores == 2:
                across(kind, z - k).start()

        @pl.when((z + k < stages) & takes)
        def _():
            along(kind, z + k, 0).wait_recv()

            @pl.when(to_left(kind))
            def _():
                along(kind, z + k, 0).start()

            if cores == 2:
                across(kind, z + k).start()

    lanes = 128

    def column(row):
        return jnp.transpose(jnp.broadcast_to(row, (lanes, rows)))[:, 0:1]

    ratios = combine_ref[...].astype(F32)
    ratio_home, ratio_away = column(ratios[0:1, :]), column(ratios[1:2, :])
    ratio_sum = ratio_home + ratio_away
    real = lax.broadcasted_iota(jnp.int32, (rows, 1), 0) < counts_ref[...]
    share_home = jnp.where(real, ratio_home / ratio_sum, 0.0)
    share_away = jnp.where(real, ratio_away / ratio_sum, 0.0)
    partner = column(partner_ref[...].astype(F32))
    chosen = partner == lax.broadcasted_iota(jnp.int32, (rows, lanes), 1).astype(F32)
    chosen = jnp.where(chosen, 1.0, 0.0)
    earlier = lax.broadcasted_iota(jnp.int32, (rows, rows), 0) > lax.broadcasted_iota(
        jnp.int32, (rows, rows), 1
    )
    earlier = jnp.where(earlier, 1.0, 0.0).astype(BF16)
    rank = jnp.sum(dot(earlier, chosen.astype(BF16)) * chosen, axis=1, keepdims=True)
    slot = partner * cap + rank
    slot_row = jnp.transpose(jnp.broadcast_to(slot, (rows, lanes)))[0:1, :]
    place_t[...] = jnp.where(
        slot == lax.broadcasted_iota(jnp.int32, (rows, away), 1).astype(F32), 1.0, 0.0
    ).astype(BF16)
    place = jnp.where(
        slot_row == lax.broadcasted_iota(jnp.int32, (away, rows), 0).astype(F32), 1.0, 0.0
    ).astype(BF16)

    def prepare(i):
        cols = pl.ds(pl.multiple_of(i * TILE, TILE), TILE)
        x = tok_ref[:, cols]
        upstream = cot_ref[:, cols].astype(F32)
        x_all[0:rows, cols] = x
        q_all[0:rows, cols] = (upstream * share_home).astype(BF16)
        send_x[:, cols] = dot(place, x).astype(BF16)
        send_q[:, cols] = dot(place, (upstream * share_away).astype(BF16)).astype(BF16)
        if padded > total:
            q_all[total:padded, cols] = jnp.zeros((padded - total, TILE), BF16)
            if hosting:
                guest_q[total:padded, cols] = jnp.zeros((padded - total, TILE), BF16)

    each(0, width // TILE, prepare)

    def slots(index, base=0):
        return pl.ds(pl.multiple_of(base + index * cap, 16), cap)

    def row_copy(which, other, block):
        return pltpu.make_async_remote_copy(
            src_ref=(send_x, send_q)[which].at[slots(other)],
            dst_ref=(x_all, q_all)[which].at[slots(block, rows)],
            send_sem=row_send.at[which, other],
            recv_sem=row_recv.at[which, block],
            device_id=(other, me_r),
            device_id_type=MESH,
        )

    def row_copy_local(which):
        return pltpu.make_async_copy(
            (send_x, send_q)[which].at[slots(me_e)],
            (x_all, q_all)[which].at[slots(me_e, rows)],
            row_local.at[which],
        )

    for which in (0, 1):
        each(1, experts, lambda i: row_copy(which, (me_e + i) % experts, me_e).start())
        row_copy_local(which).start()

    def guest_copy(index):
        if index >= 2:
            span = pl.ds(tile_order[index - 2] * TILE, TILE)
            source, target = hid_t.at[span], guest_hid_t.at[span]
        else:
            span = slice(0, rows) if index == 0 else slice(rows, total)
            source, target = q_all.at[span], guest_q.at[span]
        return pltpu.make_async_remote_copy(
            src_ref=source,
            dst_ref=target,
            send_sem=guest_send.at[index],
            recv_sem=guest_recv.at[index],
            device_id=at_stage(beside),
            device_id_type=MESH,
        )

    def hosted_copy():
        return pltpu.make_async_remote_copy(
            src_ref=guest_grad,
            dst_ref=hosted_grad,
            send_sem=hosted_send,
            recv_sem=hosted_recv,
            device_id=at_stage(beside),
            device_id_type=MESH,
        )

    def rows_arrive():
        for which in (1, 0):
            def arrive(i):
                other = (me_e + i) % experts
                row_copy(which, other, other).wait_recv()

            each(1, experts, arrive)
            row_copy_local(which).wait()
            if hosting and which == 1:
                @pl.when(outer)
                def _():
                    guest_copy(1).start()

    if hosting:
        @pl.when(outer)
        def _():
            guest_copy(0).start()
            rows_arrive()

    def travel(phase, k):
        for kind in phases[phase]:
            pass_on(kind, k)
        if phase < 2:
            start_own(phase + 1, k)

    def landed(phase):
        for kind in phases[phase]:
            local_weight(kind).wait()
            if cores == 2:
                @pl.when(inner | (kind < down))
                def _():
                    each(0, stages, lambda s: across(kind, s, owner=1 - core).wait_recv())

    each(1, stages, lambda k: travel(0, k))

    if hosting:
        pl.when(inner)(rows_arrive)
    else:
        rows_arrive()
    if padded > total:
        hid[total:padded, :] = jnp.zeros((padded - total, TILE), F32)

    def forward(tile):
        cols = slice(tile * TILE, (tile + 1) * TILE)
        x = x_all[...]
        gate = dot(x, wg[:, cols])
        up = dot(x, wu[:, cols])
        gate_act[:, cols] = gate
        up_act[:, cols] = up
        hid[0:total, :] = gate * jax.nn.sigmoid(gate) * up
        hid_t[cols, :] = jnp.transpose(hid[...]).astype(BF16)

    for phase in (0, 1):
        if phase == 1:
            each(1, stages, lambda k: travel(1, k))
        landed(phase)
        for order, tile in enumerate(tile_order):
            if 2 * order in phases[phase]:
                forward(tile)
                if hosting:
                    pl.when(outer)(lambda: guest_copy(2 + order).start())

    def pair_copy(stage):
        return pltpu.make_async_remote_copy(
            src_ref=pair_send.at[stage],
            dst_ref=pair_recv.at[stage],
            send_sem=pair_send_sem.at[stage],
            recv_sem=pair_recv_sem.at[stage],
            device_id=sibling,
            device_id_type=MESH,
        )

    def partials(stage_of, count):
        def product(i):
            stage = stage_of(i)
            length = cores * shard
            span = pl.ds(pl.multiple_of(stage * length, 16), length)

            def columns(i):
                cols = pl.ds(pl.multiple_of(i * 2 * TILE, TILE), 2 * TILE)
                value = dot(hid_t[span, :], q_all[:, cols])
                if hosting:
                    value = value + dot(guest_hid_t[span, :], guest_q[:, cols])
                for owner in range(cores):
                    pair_sum[owner, :, cols] = value[owner * shard : (owner + 1) * shard]

            each(0, width // (2 * TILE), columns)
            own_sum[stage] = pair_sum[core]
            if cores == 2:
                pair_send[stage] = pair_sum[1 - core].astype(BF16)
                pair_copy(stage).start()

        each(0, count, product)
        if cores == 2:
            def joined(i):
                stage = stage_of(i)
                pair_copy(stage).wait_recv()
                own_sum[stage] = own_sum[stage] + pair_recv[stage].astype(F32)

            each(0, count, joined)

    def sum_copy(target, way):
        there = z - 1 if way == 0 else z + 1
        slot_there = target if way == 0 else jnp.where(target == there, stages, target)
        return pltpu.make_async_remote_copy(
            src_ref=sum_send.at[target],
            dst_ref=sum_recv.at[slot_there],
            send_sem=sum_send_sem.at[target],
            recv_sem=sum_recv_sem.at[slot_there],
            device_id=at_stage(there),
            device_id_type=MESH,
        )

    def sum_arrived(slot_here):
        pltpu.make_async_remote_copy(
            src_ref=sum_send.at[0],
            dst_ref=sum_recv.at[slot_here],
            send_sem=sum_send_sem.at[0],
            recv_sem=sum_recv_sem.at[slot_here],
            device_id=at_stage(jnp.where(z > 0, z - 1, z + 1)),
            device_id_type=MESH,
        ).wait_recv()

    def chain(j, at_end):
        low, high = j, stages - 1 - j

        @pl.when((low < z) & ((z == last) == at_end) & inner)
        def _():
            value = own_sum[low]
            if not at_end:
                sum_arrived(low)
                value = value + sum_recv[low].astype(F32)
            sum_send[low] = value.astype(BF16)
            sum_copy(low, 0).start()

        @pl.when((high > z) & ((z == first) == at_end) & inner)
        def _():
            value = own_sum[high]
            if not at_end:
                sum_arrived(high)
                value = value + sum_recv[high].astype(F32)
            sum_send[high] = value.astype(BF16)
            sum_copy(high, 1).start()

    if hosting:
        travel(2, 1)

        @pl.when(inner)
        def _():
            for index in range(4):
                guest_copy(index).wait_recv()
            partials(lambda i: i * (stages - 1), 2)
            chain(0, True)

        each(2, stages, lambda k: travel(2, k))
    else:
        partials(lambda i: i, stages)
        each(0, stages, lambda j: chain(j, True))
        each(1, stages, lambda k: travel(2, k))
    landed(2)

    def backward(i, hosted=False):
        cols = pl.ds(pl.multiple_of(i * TILE, TILE), TILE)
        if hosted:
            hidden_grad = hosted_grad[:, cols].astype(F32)
        else:
            hidden_grad = dot_rows(q_all[0:total, :], wd[cols, :])
        gate = gate_act[:, cols]
        s = jax.nn.sigmoid(gate)
        gate_grad[:, cols] = (
            hidden_grad * up_act[:, cols] * s * (1.0 + gate * (1.0 - s))
        ).astype(BF16)
        up_grad[:, cols] = (hidden_grad * (gate * s)).astype(BF16)

    def for_guest(i):
        cols = pl.ds(pl.multiple_of(i * TILE, TILE), TILE)
        guest_grad[:, cols] = dot_rows(guest_q[0:total, :], wd[cols, :]).astype(BF16)

    if hosting:
        @pl.when(inner)
        def _():
            each(0, units // TILE, for_guest)
            hosted_copy().start()
            chain(0, False)
            each(0, units // TILE, backward)

        @pl.when(outer)
        def _():
            hosted_copy().wait_recv()
            each(0, units // TILE, lambda i: backward(i, True))
    else:
        each(0, units // TILE, backward)

    def inputs(i):
        cols = pl.ds(pl.multiple_of(i * TILE, TILE), TILE)
        value = dot_rows(gate_grad[...], wg[cols, :]) + dot_rows(up_grad[...], wu[cols, :])
        home[:, cols] = value[0:rows]
        back_send[:, cols] = value[rows:total].astype(BF16)

    half = width // 2

    def back_copy(part, other, block):
        cols = pl.ds(part * half, half)
        return pltpu.make_async_remote_copy(
            src_ref=back_send.at[slots(other), cols],
            dst_ref=back_recv.at[slots(block), cols],
            send_sem=back_send_sem.at[part, other],
            recv_sem=back_recv_sem.at[part, block],
            device_id=(other, me_r),
            device_id_type=MESH,
        )

    def back_copy_local(part):
        cols = pl.ds(part * half, half)
        return pltpu.make_async_copy(
            back_send.at[slots(me_e), cols],
            back_recv.at[slots(me_e), cols],
            back_local.at[part],
        )

    tiles = half // TILE
    for part_ in (0, 1):
        each(part_ * tiles, (part_ + 1) * tiles, inputs)
        each(1, experts, lambda i: back_copy(part_, (me_e + i) % experts, me_e).start())
        back_copy_local(part_).start()

    if hosting:
        @pl.when(inner)
        def _():
            guest_copy(4).wait_recv()
            partials(lambda i: i + 1, stages - 2)
            chain(1, True)
            chain(1, False)
    else:
        each(0, stages, lambda j: chain(j, False))

    def finish(i):
        cols = pl.ds(pl.multiple_of(i * TILE, TILE), TILE)
        grad_ref[:, cols] = (
            home[:, cols] + dot(place_t[...], back_recv[:, cols])
        ).astype(BF16)

    for part_ in (0, 1):
        def back_arrive(i):
            other = (me_e + i) % experts
            back_copy(part_, other, other).wait_recv()

        each(1, experts, back_arrive)
        back_copy_local(part_).wait()
        each(part_ * tiles, (part_ + 1) * tiles, finish)

    if hosting:
        @pl.when(outer)
        def _():
            own_sum[z] = jnp.zeros(own_sum.shape[1:], F32)

    @pl.when(z < last)
    def _():
        sum_arrived(z)
        own_sum[z] = own_sum[z] + sum_recv[z].astype(F32)

    @pl.when(z > first)
    def _():
        sum_arrived(stages)
        own_sum[z] = own_sum[z] + sum_recv[stages].astype(F32)

    down_ref[0] = own_sum[z].astype(BF16)

    for kind in range(down + 1):
        def sent(stage):
            @pl.when((stage >= z) & to_left(kind))
            def _():
                along(kind, stage, 0).wait_send()

            @pl.when((stage <= z) & to_right(kind))
            def _():
                along(kind, stage, 1).wait_send()

            if cores == 2:
                @pl.when(inner | (kind < down))
                def _():
                    across(kind, stage).wait_send()

        each(0, stages, sent)
    for which in (0, 1):
        each(1, experts, lambda i: row_copy(which, (me_e + i) % experts, me_e).wait_send())
        each(1, experts, lambda i: back_copy(which, (me_e + i) % experts, me_e).wait_send())

    def sums_sent(stage):
        if cores == 2:
            pair_copy(stage).wait_send()

        @pl.when(stage < z)
        def _():
            sum_copy(stage, 0).wait_send()

        @pl.when(stage > z)
        def _():
            sum_copy(stage, 1).wait_send()

    if hosting:
        @pl.when(inner)
        def _():
            each(0, stages, sums_sent)
            hosted_copy().wait_send()

        @pl.when(outer)
        def _():
            for index in range(5):
                guest_copy(index).wait_send()
    else:
        each(0, stages, sums_sent)


def local(cores, tokens, cotangent, partner, combine, counts, w_gate, w_up, w_down):
    rows, width = tokens.shape
    experts = lax.axis_size("expert")
    replicas = lax.axis_size("replica")
    stages = replicas // cores
    slots = max(2, (5 * rows // 4 + experts - 1) // experts)
    cap = -(-slots // 16) * 16
    away = experts * cap
    total = rows + away
    padded = -(-total // 128) * 128
    units = w_gate.shape[2]
    hosting = stages == 4 and units == 3 * TILE
    pieces = 2 * (units // TILE) + 1
    shard = w_down.shape[1]
    dma = pltpu.SemaphoreType.DMA
    pairs = stages if cores == 2 else 1
    in_vmem = pl.BlockSpec(memory_space=pltpu.VMEM)
    in_place = pl.BlockSpec(memory_space=pl.ANY)
    return pl.pallas_call(
        functools.partial(kernel, experts, stages, cores, cap, hosting),
        out_shape=(
            jax.ShapeDtypeStruct((rows, width), BF16),
            jax.ShapeDtypeStruct((1, shard, width), BF16),
        ),
        in_specs=[in_vmem] * 5 + [in_place] * 3,
        out_specs=(in_vmem, in_vmem),
        scratch_shapes=[
            pltpu.VMEM((width, units), BF16),
            pltpu.VMEM((width, units), BF16),
            pltpu.VMEM((units, width), BF16),
            pltpu.VMEM((total, width), BF16),
            pltpu.VMEM((padded, width), BF16),
            pltpu.VMEM((away, width), BF16),
            pltpu.VMEM((away, width), BF16),
            pltpu.VMEM((total, units), F32),
            pltpu.VMEM((total, units), F32),
            pltpu.VMEM((padded, TILE), F32),
            pltpu.VMEM((units, padded), BF16),
            pltpu.VMEM((total, units), BF16),
            pltpu.VMEM((total, units), BF16),
            pltpu.VMEM((rows, width), F32),
            pltpu.VMEM((away, width), BF16),
            pltpu.VMEM((away, width), BF16),
            pltpu.VMEM((rows, away), BF16),
            pltpu.VMEM((stages, shard, width), F32),
            pltpu.VMEM((cores, shard, width), F32),
            pltpu.VMEM((pairs, shard, width), BF16),
            pltpu.VMEM((pairs, shard, width), BF16),
            pltpu.VMEM((stages, shard, width), BF16),
            pltpu.VMEM((stages + 1, shard, width), BF16),
            pltpu.VMEM((padded if hosting else 16, width), BF16),
            pltpu.VMEM((units if hosting else 16, padded), BF16),
            pltpu.VMEM((total if hosting else 16, units), BF16),
            pltpu.VMEM((total if hosting else 16, units), BF16),
            dma((pieces,)),
            dma((pieces, stages, 2)),
            dma((pieces, stages)),
            dma((pieces, stages)),
            dma((pieces, stages)),
            dma((2, experts)),
            dma((2, experts)),
            dma((2,)),
            dma((2, experts)),
            dma((2, experts)),
            dma((2,)),
            dma((stages,)),
            dma((stages,)),
            dma((stages,)),
            dma((stages + 1,)),
            dma((5,)),
            dma((5,)),
            dma,
            dma,
        ],
        compiler_params=pltpu.CompilerParams(
            collective_id=0,
            has_side_effects=True,
            vmem_limit_bytes=60 * 2**20,
        ),
        cost_estimate=pl.CostEstimate(
            flops=12 * total * width * units,
            bytes_accessed=8 * rows * width + 6 * units * width,
            transcendentals=2 * total * units,
        ),
        name="expert_backward",
    )(tokens, cotangent, partner.T, combine.T, counts.reshape(1, 1), w_gate, w_up, w_down)


def cores_together(mesh):
    replicas = mesh.shape["replica"]
    if replicas % 2:
        return 1
    line = list(mesh.devices.reshape(-1)[:2])
    places = [getattr(device, "coords", None) for device in line]
    if None in places:
        return 2
    return 2 if tuple(places[0]) == tuple(places[1]) else 1


def solution(mesh):
    placed = (
        P(("expert", "replica"), None),
        P(("expert", "replica"), None),
        P(("expert", "replica"), None),
        P(("expert", "replica"), None),
        P(("expert", "replica")),
        P("expert", "replica", None),
        P("expert", "replica", None),
        P("expert", "replica", None),
    )
    return jax.shard_map(
        functools.partial(local, cores_together(mesh)),
        mesh=mesh,
        in_specs=placed,
        out_specs=(P(("expert", "replica"), None), P("expert", "replica", None)),
        check_vma=False,
    )
```

```python
import functools

import jax
import jax.numpy as jnp
from jax import lax
from jax.experimental import pallas as pl
from jax.experimental.pallas import tpu as pltpu
from jax.sharding import PartitionSpec as P

BF16 = jnp.bfloat16
F32 = jnp.float32
MESH = pl.DeviceIdType.MESH
TILE = 256


def dot(left, right):
    return jnp.dot(left, right, preferred_element_type=F32)


def dot_rows(left, right):
    return lax.dot_general(
        left, right, (((1,), (1,)), ((), ())), preferred_element_type=F32
    )


def each(start, stop, body):
    def step(i, carry):
        body(i)
        return carry

    lax.fori_loop(start, stop, step, 0)


def kernel(
    experts, stages, cores, cap, hosting,
    tok_ref, cot_ref, partner_ref, combine_ref, counts_ref, wg_ref, wu_ref, wd_ref,
    grad_ref, down_ref,
    wg, wu, wd, x_all, q_all, send_x, send_q, gate_act, up_act, hid, hid_t,
    gate_grad, up_grad, home, back_send, back_recv, place_t,
    own_sum, pair_sum, pair_send, pair_recv, sum_send, sum_recv,
    guest_q, guest_hid_t, guest_grad, hosted_grad,
    w_local, w_send, w_recv, w_pair_send, w_pair_recv,
    row_send, row_recv, row_local, back_send_sem, back_recv_sem, back_local,
    pair_send_sem, pair_recv_sem, sum_send_sem, sum_recv_sem,
    guest_send, guest_recv, hosted_send, hosted_recv,
):
    rows = tok_ref.shape[0]
    width = tok_ref.shape[1]
    away = experts * cap
    total = rows + away
    padded = hid.shape[0]
    units = wd.shape[0]
    shard = wd_ref.shape[1]
    me_e = lax.axis_index("expert")
    me_r = lax.axis_index("replica")
    z = me_r // cores
    core = me_r % cores
    tiles_h = units // TILE
    tile_order = [0] + [tiles_h - 1] * (tiles_h > 1) + list(range(1, tiles_h - 1))
    pieces = [(which, tile) for tile in tile_order for which in (0, 1)] + [(2, 0)]
    down = len(pieces) - 1
    early = min(4, down)
    phases = (range(0, early), range(early, down), range(down, down + 1))

    def at_stage(stage):
        return (me_e, stage * cores + core)

    sibling = (me_e, z * cores + (cores - 1 - core))
    first, last = (1, stages - 2) if hosting else (0, stages - 1)
    inner = (z >= first) & (z <= last)
    outer = (z < first) | (z > last)
    beside = jnp.where(z == 0, 1, jnp.where(z == stages - 1, stages - 2,
                       jnp.where(z == 1, 0, stages - 1)))

    def to_left(kind):
        return z > (first if kind == down else 0)

    def to_right(kind):
        return z < (last if kind == down else stages - 1)

    barrier = pltpu.get_barrier_semaphore()

    def greet(device):
        pl.semaphore_signal(barrier, inc=1, device_id=device, device_id_type=MESH)

    @pl.when(z > 0)
    def _():
        greet(at_stage(z - 1))

    @pl.when(z < stages - 1)
    def _():
        greet(at_stage(z + 1))

    if cores == 2:
        greet(sibling)

    each(1, experts, lambda i: greet(((me_e + i) % experts, me_r)))
    ends = jnp.where(z > 0, 1, 0) + jnp.where(z < stages - 1, 1, 0)
    pl.semaphore_wait(barrier, ends + (cores - 1) + (experts - 1))

    def part(kind, stage, owner_core):
        which, tile = pieces[kind]
        length = (wg_ref, wu_ref, wd_ref)[which].shape[1]
        begin = pl.multiple_of((stage * cores + owner_core) * length, 16)
        span = pl.ds(begin, length)
        if kind == down:
            return wd.at[span]
        return (wg, wu)[which].at[span, pl.ds(tile * TILE, TILE)]

    def mine(kind):
        which, tile = pieces[kind]
        if kind == down:
            return wd_ref.at[0]
        return (wg_ref, wu_ref)[which].at[0, :, pl.ds(tile * TILE, TILE)]

    def along(kind, stage, way, own=False):
        return pltpu.make_async_remote_copy(
            src_ref=mine(kind) if own else part(kind, stage, core),
            dst_ref=part(kind, stage, core),
            send_sem=w_send.at[kind, stage, way],
            recv_sem=w_recv.at[kind, stage],
            device_id=at_stage(z - 1 if way == 0 else z + 1),
            device_id_type=MESH,
        )

    def across(kind, stage, own=False, owner=None):
        owner = core if owner is None else owner
        return pltpu.make_async_remote_copy(
            src_ref=mine(kind) if own else part(kind, stage, owner),
            dst_ref=part(kind, stage, owner),
            send_sem=w_pair_send.at[kind, stage],
            recv_sem=w_pair_recv.at[kind, stage],
            device_id=sibling,
            device_id_type=MESH,
        )

    def local_weight(kind):
        return pltpu.make_async_copy(
            mine(kind), part(kind, z, core), w_local.at[kind]
        )

    def start_own(phase, k):
        for kind in phases[phase]:
            @pl.when(to_left(kind) & (stages - 1 - z == k))
            def _():
                along(kind, z, 0, True).start()

            @pl.when(to_right(kind) & (z == k))
            def _():
                along(kind, z, 1, True).start()

    for kind in phases[0]:
        @pl.when(to_left(kind))
        def _():
            along(kind, z, 0, True).start()

        @pl.when(to_right(kind))
        def _():
            along(kind, z, 1, True).start()

    start_own(1, 0)
    start_own(2, 0)
    for kind in range(down + 1):
        if cores == 2:
            @pl.when(inner | (kind < down))
            def _():
                across(kind, z, True).start()

        local_weight(kind).start()

    def pass_on(kind, k):
        takes = inner | (kind < down)

        @pl.when((z - k >= 0) & takes)
        def _():
            along(kind, z - k, 1).wait_recv()

            @pl.when(to_right(kind))
            def _():
                along(kind, z - k, 1).start()

            if cores == 2:
                across(kind, z - k).start()

        @pl.when((z + k < stages) & takes)
        def _():
            along(kind, z + k, 0).wait_recv()

            @pl.when(to_left(kind))
            def _():
                along(kind, z + k, 0).start()

            if cores == 2:
                across(kind, z + k).start()

    lanes = 128

    def column(row):
        return jnp.transpose(jnp.broadcast_to(row, (lanes, rows)))[:, 0:1]

    ratios = combine_ref[...].astype(F32)
    ratio_home, ratio_away = column(ratios[0:1, :]), column(ratios[1:2, :])
    ratio_sum = ratio_home + ratio_away
    real = lax.broadcasted_iota(jnp.int32, (rows, 1), 0) < counts_ref[...]
    share_home = jnp.where(real, ratio_home / ratio_sum, 0.0)
    share_away = jnp.where(real, ratio_away / ratio_sum, 0.0)
    partner = column(partner_ref[...].astype(F32))
    chosen = partner == lax.broadcasted_iota(jnp.int32, (rows, lanes), 1).astype(F32)
    chosen = jnp.where(chosen, 1.0, 0.0)
    earlier = lax.broadcasted_iota(jnp.int32, (rows, rows), 0) > lax.broadcasted_iota(
        jnp.int32, (rows, rows), 1
    )
    earlier = jnp.where(earlier, 1.0, 0.0).astype(BF16)
    rank = jnp.sum(dot(earlier, chosen.astype(BF16)) * chosen, axis=1, keepdims=True)
    slot = partner * cap + rank
    slot_row = jnp.transpose(jnp.broadcast_to(slot, (rows, lanes)))[0:1, :]
    place_t[...] = jnp.where(
        slot == lax.broadcasted_iota(jnp.int32, (rows, away), 1).astype(F32), 1.0, 0.0
    ).astype(BF16)
    place = jnp.where(
        slot_row == lax.broadcasted_iota(jnp.int32, (away, rows), 0).astype(F32), 1.0, 0.0
    ).astype(BF16)

    def prepare(i):
        cols = pl.ds(pl.multiple_of(i * TILE, TILE), TILE)
        x = tok_ref[:, cols]
        upstream = cot_ref[:, cols].astype(F32)
        x_all[0:rows, cols] = x
        q_all[0:rows, cols] = (upstream * share_home).astype(BF16)
        send_x[:, cols] = dot(place, x).astype(BF16)
        send_q[:, cols] = dot(place, (upstream * share_away).astype(BF16)).astype(BF16)
        if padded > total:
            q_all[total:padded, cols] = jnp.zeros((padded - total, TILE), BF16)
            if hosting:
                guest_q[total:padded, cols] = jnp.zeros((padded - total, TILE), BF16)

    each(0, width // TILE, prepare)

    def slots(index, base=0):
        return pl.ds(pl.multiple_of(base + index * cap, 16), cap)

    def row_copy(which, other, block):
        return pltpu.make_async_remote_copy(
            src_ref=(send_x, send_q)[which].at[slots(other)],
            dst_ref=(x_all, q_all)[which].at[slots(block, rows)],
            send_sem=row_send.at[which, other],
            recv_sem=row_recv.at[which, block],
            device_id=(other, me_r),
            device_id_type=MESH,
        )

    def row_copy_local(which):
        return pltpu.make_async_copy(
            (send_x, send_q)[which].at[slots(me_e)],
            (x_all, q_all)[which].at[slots(me_e, rows)],
            row_local.at[which],
        )

    for which in (0, 1):
        each(1, experts, lambda i: row_copy(which, (me_e + i) % experts, me_e).start())
        row_copy_local(which).start()

    def guest_copy(index):
        if index >= 2:
            span = pl.ds(tile_order[index - 2] * TILE, TILE)
            source, target = hid_t.at[span], guest_hid_t.at[span]
        else:
            span = slice(0, rows) if index == 0 else slice(rows, total)
            source, target = q_all.at[span], guest_q.at[span]
        return pltpu.make_async_remote_copy(
            src_ref=source,
            dst_ref=target,
            send_sem=guest_send.at[index],
            recv_sem=guest_recv.at[index],
            device_id=at_stage(beside),
            device_id_type=MESH,
        )

    def hosted_copy(tile):
        cols = pl.ds(tile * TILE, TILE)
        return pltpu.make_async_remote_copy(
            src_ref=guest_grad.at[:, cols],
            dst_ref=hosted_grad.at[:, cols],
            send_sem=hosted_send.at[tile],
            recv_sem=hosted_recv.at[tile],
            device_id=at_stage(beside),
            device_id_type=MESH,
        )

    def rows_arrive():
        for which in (1, 0):
            def arrive(i):
                other = (me_e + i) % experts
                row_copy(which, other, other).wait_recv()

            each(1, experts, arrive)
            row_copy_local(which).wait()
            if hosting and which == 1:
                @pl.when(outer)
                def _():
                    guest_copy(1).start()

    if hosting:
        @pl.when(outer)
        def _():
            guest_copy(0).start()
            rows_arrive()

    def travel(phase, k):
        for kind in phases[phase]:
            pass_on(kind, k)
        if phase < 2:
            start_own(phase + 1, k)

    def landed(phase):
        for kind in phases[phase]:
            local_weight(kind).wait()
            if cores == 2:
                @pl.when(inner | (kind < down))
                def _():
                    each(0, stages, lambda s: across(kind, s, owner=1 - core).wait_recv())

    each(1, stages, lambda k: travel(0, k))

    if hosting:
        pl.when(inner)(rows_arrive)
    else:
        rows_arrive()
    if padded > total:
        hid[total:padded, :] = jnp.zeros((padded - total, TILE), F32)

    def forward(tile):
        cols = slice(tile * TILE, (tile + 1) * TILE)
        x = x_all[...]
        gate = dot(x, wg[:, cols])
        up = dot(x, wu[:, cols])
        gate_act[:, cols] = gate
        up_act[:, cols] = up
        hid[0:total, :] = gate * jax.nn.sigmoid(gate) * up
        hid_t[cols, :] = jnp.transpose(hid[...]).astype(BF16)

    for phase in (0, 1):
        if phase == 1:
            each(1, stages, lambda k: travel(1, k))
        landed(phase)
        for order, tile in enumerate(tile_order):
            if 2 * order in phases[phase]:
                forward(tile)
                if hosting:
                    pl.when(outer)(lambda: guest_copy(2 + order).start())

    def pair_copy(stage):
        return pltpu.make_async_remote_copy(
            src_ref=pair_send.at[stage],
            dst_ref=pair_recv.at[stage],
            send_sem=pair_send_sem.at[stage],
            recv_sem=pair_recv_sem.at[stage],
            device_id=sibling,
            device_id_type=MESH,
        )

    def partials(stage_of, count):
        def product(i):
            stage = stage_of(i)
            length = cores * shard
            span = pl.ds(pl.multiple_of(stage * length, 16), length)

            def columns(i):
                cols = pl.ds(pl.multiple_of(i * 2 * TILE, TILE), 2 * TILE)
                value = dot(hid_t[span, :], q_all[:, cols])
                if hosting:
                    value = value + dot(guest_hid_t[span, :], guest_q[:, cols])
                for owner in range(cores):
                    pair_sum[owner, :, cols] = value[owner * shard : (owner + 1) * shard]

            each(0, width // (2 * TILE), columns)
            own_sum[stage] = pair_sum[core]
            if cores == 2:
                pair_send[stage] = pair_sum[1 - core].astype(BF16)
                pair_copy(stage).start()

        each(0, count, product)
        if cores == 2:
            def joined(i):
                stage = stage_of(i)
                pair_copy(stage).wait_recv()
                own_sum[stage] = own_sum[stage] + pair_recv[stage].astype(F32)

            each(0, count, joined)

    def sum_copy(target, way):
        there = z - 1 if way == 0 else z + 1
        slot_there = target if way == 0 else jnp.where(target == there, stages, target)
        return pltpu.make_async_remote_copy(
            src_ref=sum_send.at[target],
            dst_ref=sum_recv.at[slot_there],
            send_sem=sum_send_sem.at[target],
            recv_sem=sum_recv_sem.at[slot_there],
            device_id=at_stage(there),
            device_id_type=MESH,
        )

    def sum_arrived(slot_here):
        pltpu.make_async_remote_copy(
            src_ref=sum_send.at[0],
            dst_ref=sum_recv.at[slot_here],
            send_sem=sum_send_sem.at[0],
            recv_sem=sum_recv_sem.at[slot_here],
            device_id=at_stage(jnp.where(z > 0, z - 1, z + 1)),
            device_id_type=MESH,
        ).wait_recv()

    def chain(j, at_end):
        low, high = j, stages - 1 - j

        @pl.when((low < z) & ((z == last) == at_end) & inner)
        def _():
            value = own_sum[low]
            if not at_end:
                sum_arrived(low)
                value = value + sum_recv[low].astype(F32)
            sum_send[low] = value.astype(BF16)
            sum_copy(low, 0).start()

        @pl.when((high > z) & ((z == first) == at_end) & inner)
        def _():
            value = own_sum[high]
            if not at_end:
                sum_arrived(high)
                value = value + sum_recv[high].astype(F32)
            sum_send[high] = value.astype(BF16)
            sum_copy(high, 1).start()

    if hosting:
        each(1, stages, lambda k: travel(2, k))
    else:
        partials(lambda i: i, stages)
        each(0, stages, lambda j: chain(j, True))
        each(1, stages, lambda k: travel(2, k))
    landed(2)

    def backward(i, hosted=False):
        cols = pl.ds(i * TILE, TILE) if hosted else pl.ds(pl.multiple_of(i * TILE, TILE), TILE)
        if hosted:
            hidden_grad = hosted_grad[:, cols].astype(F32)
        else:
            hidden_grad = dot_rows(q_all[0:total, :], wd[cols, :])
        gate = gate_act[:, cols]
        s = jax.nn.sigmoid(gate)
        gate_grad[:, cols] = (
            hidden_grad * up_act[:, cols] * s * (1.0 + gate * (1.0 - s))
        ).astype(BF16)
        up_grad[:, cols] = (hidden_grad * (gate * s)).astype(BF16)

    def for_guest(i):
        cols = pl.ds(i * TILE, TILE)
        guest_grad[:, cols] = dot_rows(guest_q[0:total, :], wd[cols, :]).astype(BF16)

    if hosting:
        @pl.when(inner)
        def _():
            guest_copy(0).wait_recv()
            guest_copy(1).wait_recv()
            for tile in range(tiles_h):
                for_guest(tile)
                hosted_copy(tile).start()
            guest_copy(2).wait_recv()
            guest_copy(3).wait_recv()
            partials(lambda i: i * (stages - 1), 2)
            chain(0, True)
            each(0, units // TILE, backward)

        @pl.when(outer)
        def _():
            for tile in range(tiles_h):
                hosted_copy(tile).wait_recv()
                backward(tile, True)
    else:
        each(0, units // TILE, backward)

    def inputs(i):
        cols = pl.ds(pl.multiple_of(i * TILE, TILE), TILE)
        value = dot_rows(gate_grad[...], wg[cols, :]) + dot_rows(up_grad[...], wu[cols, :])
        home[:, cols] = value[0:rows]
        back_send[:, cols] = value[rows:total].astype(BF16)

    half = width // 2

    def back_copy(part, other, block):
        cols = pl.ds(part * half, half)
        return pltpu.make_async_remote_copy(
            src_ref=back_send.at[slots(other), cols],
            dst_ref=back_recv.at[slots(block), cols],
            send_sem=back_send_sem.at[part, other],
            recv_sem=back_recv_sem.at[part, block],
            device_id=(other, me_r),
            device_id_type=MESH,
        )

    def back_copy_local(part):
        cols = pl.ds(part * half, half)
        return pltpu.make_async_copy(
            back_send.at[slots(me_e), cols],
            back_recv.at[slots(me_e), cols],
            back_local.at[part],
        )

    tiles = half // TILE
    for part_ in (0, 1):
        each(part_ * tiles, (part_ + 1) * tiles, inputs)
        each(1, experts, lambda i: back_copy(part_, (me_e + i) % experts, me_e).start())
        back_copy_local(part_).start()
        if hosting and part_ == 0:
            @pl.when(inner)
            def _():
                chain(0, False)

    if hosting:
        @pl.when(inner)
        def _():
            guest_copy(4).wait_recv()
            partials(lambda i: i + 1, stages - 2)
            chain(1, True)
            chain(1, False)
    else:
        each(0, stages, lambda j: chain(j, False))

    def finish(i):
        cols = pl.ds(pl.multiple_of(i * TILE, TILE), TILE)
        grad_ref[:, cols] = (
            home[:, cols] + dot(place_t[...], back_recv[:, cols])
        ).astype(BF16)

    for part_ in (0, 1):
        def back_arrive(i):
            other = (me_e + i) % experts
            back_copy(part_, other, other).wait_recv()

        each(1, experts, back_arrive)
        back_copy_local(part_).wait()
        each(part_ * tiles, (part_ + 1) * tiles, finish)

    if hosting:
        @pl.when(outer)
        def _():
            own_sum[z] = jnp.zeros(own_sum.shape[1:], F32)

    @pl.when(z < last)
    def _():
        sum_arrived(z)
        own_sum[z] = own_sum[z] + sum_recv[z].astype(F32)

    @pl.when(z > first)
    def _():
        sum_arrived(stages)
        own_sum[z] = own_sum[z] + sum_recv[stages].astype(F32)

    down_ref[0] = own_sum[z].astype(BF16)

    for kind in range(down + 1):
        def sent(stage):
            @pl.when((stage >= z) & to_left(kind))
            def _():
                along(kind, stage, 0).wait_send()

            @pl.when((stage <= z) & to_right(kind))
            def _():
                along(kind, stage, 1).wait_send()

            if cores == 2:
                @pl.when(inner | (kind < down))
                def _():
                    across(kind, stage).wait_send()

        each(0, stages, sent)
    for which in (0, 1):
        each(1, experts, lambda i: row_copy(which, (me_e + i) % experts, me_e).wait_send())
        each(1, experts, lambda i: back_copy(which, (me_e + i) % experts, me_e).wait_send())

    def sums_sent(stage):
        if cores == 2:
            pair_copy(stage).wait_send()

        @pl.when(stage < z)
        def _():
            sum_copy(stage, 0).wait_send()

        @pl.when(stage > z)
        def _():
            sum_copy(stage, 1).wait_send()

    if hosting:
        @pl.when(inner)
        def _():
            each(0, stages, sums_sent)
            for tile in range(tiles_h):
                hosted_copy(tile).wait_send()

        @pl.when(outer)
        def _():
            for index in range(5):
                guest_copy(index).wait_send()
    else:
        each(0, stages, sums_sent)


def local(cores, tokens, cotangent, partner, combine, counts, w_gate, w_up, w_down):
    rows, width = tokens.shape
    experts = lax.axis_size("expert")
    replicas = lax.axis_size("replica")
    stages = replicas // cores
    slots = max(2, (5 * rows // 4 + experts - 1) // experts)
    cap = -(-slots // 16) * 16
    away = experts * cap
    total = rows + away
    padded = -(-total // 128) * 128
    units = w_gate.shape[2]
    hosting = stages == 4 and units == 3 * TILE
    pieces = 2 * (units // TILE) + 1
    shard = w_down.shape[1]
    dma = pltpu.SemaphoreType.DMA
    pairs = stages if cores == 2 else 1
    in_vmem = pl.BlockSpec(memory_space=pltpu.VMEM)
    in_place = pl.BlockSpec(memory_space=pl.ANY)
    return pl.pallas_call(
        functools.partial(kernel, experts, stages, cores, cap, hosting),
        out_shape=(
            jax.ShapeDtypeStruct((rows, width), BF16),
            jax.ShapeDtypeStruct((1, shard, width), BF16),
        ),
        in_specs=[in_vmem] * 5 + [in_place] * 3,
        out_specs=(in_vmem, in_vmem),
        scratch_shapes=[
            pltpu.VMEM((width, units), BF16),
            pltpu.VMEM((width, units), BF16),
            pltpu.VMEM((units, width), BF16),
            pltpu.VMEM((total, width), BF16),
            pltpu.VMEM((padded, width), BF16),
            pltpu.VMEM((away, width), BF16),
            pltpu.VMEM((away, width), BF16),
            pltpu.VMEM((total, units), F32),
            pltpu.VMEM((total, units), F32),
            pltpu.VMEM((padded, TILE), F32),
            pltpu.VMEM((units, padded), BF16),
            pltpu.VMEM((total, units), BF16),
            pltpu.VMEM((total, units), BF16),
            pltpu.VMEM((rows, width), F32),
            pltpu.VMEM((away, width), BF16),
            pltpu.VMEM((away, width), BF16),
            pltpu.VMEM((rows, away), BF16),
            pltpu.VMEM((stages, shard, width), F32),
            pltpu.VMEM((cores, shard, width), F32),
            pltpu.VMEM((pairs, shard, width), BF16),
            pltpu.VMEM((pairs, shard, width), BF16),
            pltpu.VMEM((stages, shard, width), BF16),
            pltpu.VMEM((stages + 1, shard, width), BF16),
            pltpu.VMEM((padded if hosting else 16, width), BF16),
            pltpu.VMEM((units if hosting else 16, padded), BF16),
            pltpu.VMEM((total if hosting else 16, units), BF16),
            pltpu.VMEM((total if hosting else 16, units), BF16),
            dma((pieces,)),
            dma((pieces, stages, 2)),
            dma((pieces, stages)),
            dma((pieces, stages)),
            dma((pieces, stages)),
            dma((2, experts)),
            dma((2, experts)),
            dma((2,)),
            dma((2, experts)),
            dma((2, experts)),
            dma((2,)),
            dma((stages,)),
            dma((stages,)),
            dma((stages,)),
            dma((stages + 1,)),
            dma((5,)),
            dma((5,)),
            dma((3,)),
            dma((3,)),
        ],
        compiler_params=pltpu.CompilerParams(
            collective_id=0,
            has_side_effects=True,
            vmem_limit_bytes=60 * 2**20,
        ),
        cost_estimate=pl.CostEstimate(
            flops=12 * total * width * units,
            bytes_accessed=8 * rows * width + 6 * units * width,
            transcendentals=2 * total * units,
        ),
        name="expert_backward",
    )(tokens, cotangent, partner.T, combine.T, counts.reshape(1, 1), w_gate, w_up, w_down)


def cores_together(mesh):
    replicas = mesh.shape["replica"]
    if replicas % 2:
        return 1
    line = list(mesh.devices.reshape(-1)[:2])
    places = [getattr(device, "coords", None) for device in line]
    if None in places:
        return 2
    return 2 if tuple(places[0]) == tuple(places[1]) else 1


def solution(mesh):
    placed = (
        P(("expert", "replica"), None),
        P(("expert", "replica"), None),
        P(("expert", "replica"), None),
        P(("expert", "replica"), None),
        P(("expert", "replica")),
        P("expert", "replica", None),
        P("expert", "replica", None),
        P("expert", "replica", None),
    )
    return jax.shard_map(
        functools.partial(local, cores_together(mesh)),
        mesh=mesh,
        in_specs=placed,
        out_specs=(P(("expert", "replica"), None), P("expert", "replica", None)),
        check_vma=False,
    )
```
